128 devices in a mesh: reorder: 8 (over z, core), pair: 16 (over y, x).
Axes of the slice: x: 4, y: 4, z: 4, core: 2. Of those that a mesh axis runs over, the one named last changes fastest.
Arguments:
- amps: bfloat16 [16, 16, 16, 4096], P('pair', 'reorder'), may hold values from -3 to 3
- tile_index: int32 [16, 16, 16], replicated, may hold values from 0 to 625, as said below
- ovov: bfloat16 [16, 16, 16, 4096], P('pair', 'reorder'), may hold values from -6 to 6
- cycle_ints: bfloat16 [16, 16, 25, 25, 4096], P('pair', 'reorder'), may hold values from -0.25 to 0.25
- history: bfloat16 [6, 16, 16, 16, 4096], P(None, 'pair', 'reorder'), may hold values from -6 to 6
- slab: int32 [16], replicated, may hold values from 0 to 199, as said below
- eps_occ: float32 [200], replicated, may hold values from -2 to -0.5
- eps_vir: float32 [1600], replicated, may hold values from 0.3 to 4
Outputs:
- new_amps: bfloat16 [16, 16, 16, 4096], P('pair', 'reorder')
- gram_row: float32 [7], replicated
The draws below stay inside these ranges and needn't reach their ends.
Inputs may be any that keep to these rules, and one draw needn't show every extreme that they name: `tile_index`: entry (i, j, s) is a * 25 + b for the distinct tile (a, b) held in slot s of pair (i, j), or 625 for an empty slot. Live slots come first; each pair has 2 or more. At most 2 live tiles of one pair share a row a, reached. Pairs (i, 2m) and (i, 2m + 1) hold at most 24 live tiles together, reached; some pair holds 16. `slab`: distinct occupied orbitals.
All inputs are finite; a program needn't handle non-finite values.
Results may differ from the reference program's by a relative error of at most 0.008.
Values may be sent and summed in bfloat16 or wider, within the bound.
A program may use at most 128 MiB of HBM per device.

```python
import jax
import jax.numpy as jnp
from jax import lax

V = 1600
NOCC = 200
TILE = 64
NT = 25
NS = 16
CAPT = 16
ROWCAP = 2
LIVE2 = 24
NHIST = 6


def draw_tile_index(key, part):
    key = jax.random.fold_in(key, 11)
    across = V // TILE
    key_rows, key_cols, key_order, key_first, key_second, key_pick = jax.random.split(key, 6)
    pairs = NS * NS
    rows = jax.vmap(lambda k: jax.random.permutation(k, across)[:CAPT // ROWCAP])(jax.random.split(key_rows, pairs))
    rows = jnp.repeat(rows, ROWCAP, axis=1)
    cols = jax.vmap(lambda k: jax.random.permutation(k, across)[:CAPT])(jax.random.split(key_cols, pairs))
    order = jax.vmap(lambda k: jax.random.permutation(k, CAPT))(jax.random.split(key_order, pairs))
    tiles = jnp.take_along_axis(rows * across + cols, order, axis=1).reshape(NS, NS, CAPT)
    half = NS // 2
    first = jax.random.randint(key_first, (NS, half), 2, CAPT + 1)
    second_top = jnp.minimum(CAPT, LIVE2 - first) + 1
    second = jax.random.randint(key_second, (NS, half), 2, second_top)
    chosen = jax.random.randint(key_pick, (), 0, NS * half)
    places = jnp.arange(NS * half).reshape(NS, half)
    first = jnp.where(places == chosen, CAPT, first)
    second = jnp.where(places == chosen, LIVE2 - CAPT, second)
    counts = jnp.stack([first, second], axis=2).reshape(NS, NS)
    slot = jnp.arange(CAPT)
    return jnp.where(slot[None, None, :] < counts[..., None], tiles, across * across).astype(jnp.int32)


def draw_slab(key, part):
    key = jax.random.fold_in(key, 23)
    key_inner, key_order = jax.random.split(key, 2)
    inner = jax.random.permutation(key_inner, NOCC - 2)[:NS - 2] + 1
    chosen = jnp.concatenate([jnp.array([0, NOCC - 1], dtype=jnp.int32), inner.astype(jnp.int32)])
    return jax.random.permutation(key_order, chosen).astype(jnp.int32)


def block_levels(own_key, extent, shards, least, largest):
    loudness, own = 1.0, jax.random.fold_in(own_key, 6)
    for position, blocks in shards:
        heights = jnp.exp(jax.random.uniform(jax.random.fold_in(own, position), (blocks,), jnp.float32, least / len(shards), largest / len(shards)))
        loudness = loudness * jnp.repeat(heights, extent[position] // blocks).reshape([-1 if axis == position else 1 for axis in range(len(extent))])
    return loudness


def centred(stream_key, dims, scale, most, pieces=(), held_as=jnp.bfloat16):
    entries = scale * jax.random.normal(stream_key, dims, jnp.float32)
    if pieces:
        entries = entries * block_levels(stream_key, dims, pieces, -0.22, 0.18)
    return jnp.clip(entries, -most, most).astype(held_as)


def setup_inputs(seed: int = 0) -> dict:
    arg_keys = jax.random.split(jax.random.key(seed), 9)
    return {
        "amps": centred(arg_keys[0], (NS, NS, CAPT, TILE * TILE), 0.5, 3.0, ((0, 16), (1, 8))),
        "tile_index": draw_tile_index(jax.random.fold_in(arg_keys[8], 71), 0),
        "ovov": centred(arg_keys[2], (NS, NS, CAPT, TILE * TILE), 1.0, 6.0, ((0, 16), (1, 8))),
        "cycle_ints": centred(arg_keys[3], (NS, NS, NT, NT, TILE * TILE), (TILE * NS // 2) ** -0.5, 0.25, ((0, 16), (1, 8))),
        "history": centred(arg_keys[4], (NHIST, NS, NS, CAPT, TILE * TILE), 1.0, 6.0, ((1, 16), (2, 8))),
        "slab": draw_slab(jax.random.fold_in(arg_keys[8], 71), 0),
        "eps_occ": jnp.clip(jax.random.uniform(arg_keys[6], (NOCC,), jnp.float32, -2.0, -0.5), -2.0, -0.5),
        "eps_vir": jnp.clip(jax.random.uniform(arg_keys[7], (V,), jnp.float32, 0.3, 4.0), 0.3, 4.0),
    }


def match_lists(out_idx, in_idx, across):
    live_in = in_idx < across * across
    same = ((out_idx // across)[:, None] == (in_idx // across)[None, :]) & live_in[None, :]
    width = in_idx.shape[0]
    ranks = width - jnp.arange(width, dtype=jnp.int32)
    scores = jnp.where(same, ranks[None, :], jnp.zeros_like(ranks)[None, :])
    values, picks = lax.top_k(scores, ROWCAP)
    return (picks, values > 0)

def cycle_block(tiles, in_idx, ints_k, out_idx, out_pair):
    across = ints_k.shape[1]
    slots = out_idx.shape[0]
    picks, present = match_lists(out_idx, in_idx, across)
    cols_in = in_idx % across
    cols_out = out_idx % across
    left = tiles[picks].astype(jnp.float32) * present[..., None].astype(jnp.float32)
    left = left.reshape(slots, ROWCAP, TILE, TILE).transpose(0, 2, 1, 3).reshape(slots, TILE, ROWCAP * TILE)
    right = ints_k[out_pair[:, None], cols_in[picks], cols_out[:, None]].astype(jnp.float32)
    right = right.reshape(slots, ROWCAP * TILE, TILE)
    return jnp.einsum('sak,skb->sab', left, right, precision=lax.Precision.HIGHEST)

def reference(amps, tile_index, ovov, cycle_ints, history, slab, eps_occ, eps_vir):
    across = V // TILE
    live = (tile_index < across * across).astype(jnp.float32)
    rows_a = jnp.minimum(tile_index // across, across - 1)
    cols_b = tile_index % across

    def one_pair(flat):
        first = flat // NS
        second = flat % NS
        out_idx = tile_index[first, second]
        out_pair = jnp.zeros((CAPT,), jnp.int32) + second

        def add_term(total, other):
            term = cycle_block(amps[first, other], tile_index[first, other], cycle_ints[other], out_idx, out_pair)
            return (total + term, None)
        start = jnp.zeros((CAPT, TILE, TILE), jnp.float32)
        total, _ = lax.scan(add_term, start, jnp.arange(NS, dtype=jnp.int32))
        return total.reshape(CAPT, TILE * TILE)
    cycle = lax.map(one_pair, jnp.arange(NS * NS, dtype=jnp.int32)).reshape(NS, NS, CAPT, TILE * TILE)
    resid = (ovov.astype(jnp.float32) + cycle) * live[..., None]
    occ_energy = eps_occ[slab]
    vir_tiles = eps_vir.reshape(across, TILE)
    row_energy = vir_tiles[rows_a]
    col_energy = vir_tiles[cols_b]
    denom = occ_energy[:, None, None, None, None] + occ_energy[None, :, None, None, None]
    denom = denom - row_energy[..., :, None] - col_energy[..., None, :]
    denom = denom.reshape(NS, NS, CAPT, TILE * TILE)
    new_amps = ((amps.astype(jnp.float32) + resid / denom) * live[..., None]).astype(jnp.bfloat16)
    cross = jnp.einsum('hijsx,ijsx->h', history.astype(jnp.float32), resid, precision=lax.Precision.HIGHEST)
    square = jnp.sum(resid * resid)
    gram_row = jnp.concatenate([cross, jnp.sqrt(square)[None]]) / (TILE * NS)
    return (new_amps, gram_row)
```

```python
import jax
import jax.numpy as jnp
from jax import lax
from jax.experimental import pallas as pl
from jax.experimental.pallas import tpu as pltpu
from jax.sharding import PartitionSpec as P

MESH = pl.DeviceIdType.MESH
TILE = 64
HALF = 32
AREA = TILE * TILE
LIVE2 = 24
NP = 16
NR = 8
CAPT = 16
NH = 6
F32, BF16 = jnp.float32, jnp.bfloat16


def iota(shape, dim):
    return lax.broadcasted_iota(jnp.int32, shape, dim)


def kernel(
    jobs, slot_of, amps, live, pair_e, row_e, col_e, ovov_hbm, ints_hbm, hist_hbm,
    new_amps, gram,
    ints, ovov, hist, stage, a_out, a_land, a_exp, mask, parts, c_land, total, cyc, g_one, g_two,
    w_sem, in_sem, a_send, a_recv, c_send, c_recv, g_send, g_recv,
):
    r = lax.axis_index("reorder")
    p = lax.axis_index("pair")
    barrier = pltpu.get_barrier_semaphore()

    def signal(device):
        pl.semaphore_signal(barrier, inc=1, device_id=device, device_id_type=MESH)

    w_copy = pltpu.make_async_copy(ints_hbm, ints, w_sem.at[0])
    w_copy.start()
    ovov_copy = pltpu.make_async_copy(ovov_hbm, ovov, in_sem.at[0])
    ovov_copy.start()
    hist_copy = pltpu.make_async_copy(hist_hbm, hist, in_sem.at[1])
    hist_copy.start()

    def greet_row(d, c):
        signal(((r + d) % NR, p))
        return c

    def greet_pair(d, c):
        signal((r, (p + d) % NP))
        return c

    own = p // 2 == r

    def greet_amps(i, c):
        @pl.when(jnp.logical_not(jnp.logical_and(own, i == p)))
        def _():
            signal((p // 2, i))

        return c

    lax.fori_loop(1, NR, greet_row, 0)
    lax.fori_loop(1, NP, greet_pair, 0)
    lax.fori_loop(0, NP, greet_amps, 0)

    lane_in, lane_out = iota((128, 128), 0), iota((128, 128), 1)
    half, q = lane_in // TILE, lane_in % TILE
    order = (lane_out == half * TILE + (q % 2) * HALF + q // 2).astype(BF16)

    def turn(m, c):
        x = amps[:, :, pl.ds(pl.multiple_of(m * 128, 128), 128)].reshape(2 * CAPT, 128)
        y = jnp.dot(x, order, preferred_element_type=F32)
        stage[pl.ds(m, 2 * CAPT, stride=HALF), :] = y
        return c

    lax.fori_loop(0, HALF, turn, 0)
    a_out[...] = stage[...].astype(BF16).reshape(2, CAPT * HALF, 128)

    pl.semaphore_wait(barrier, NR - 1 + NP - 1 + 2 * NR - own.astype(jnp.int32))

    def amps_copy(kk, d):
        return pltpu.make_async_remote_copy(
            src_ref=a_out.at[kk],
            dst_ref=a_land.at[p],
            send_sem=a_send.at[kk * NR + d],
            recv_sem=a_recv.at[p],
            device_id=((r + d) % NR, 2 * r + kk),
            device_id_type=MESH,
        )

    def to_other(kk, d):
        return jnp.logical_not(jnp.logical_and(d == 0, 2 * r + kk == p))

    def send_amps(n, c):
        @pl.when(to_other(n % 2, n // 2))
        def _():
            amps_copy(n % 2, n // 2).start()

        return c

    lax.fori_loop(0, 2 * NR, send_amps, 0)

    @pl.when(own)
    def _():
        a_land[p] = a_out[p % 2]

    lane_in, lane_out = iota((128, 256), 0), iota((128, 256), 1)
    spread = (lane_in == lane_out // 2).astype(BF16)
    lane = iota((CAPT, 128), 1)
    mask[0] = (lane % 2 == 0).astype(BF16)
    mask[1] = (lane % 2 == 1).astype(BF16)
    mask[2] = jnp.zeros((CAPT, 128), BF16)
    low = iota((1, 128), 1) < TILE
    low_f = (iota((TILE, 128), 1) < TILE).astype(F32)
    keep = (low_f.astype(BF16), (1.0 - low_f).astype(BF16))
    low = iota((HALF, 128), 1) < TILE

    w_copy.wait()

    def parts_copy(i):
        return pltpu.make_async_remote_copy(
            src_ref=parts.at[i],
            dst_ref=c_land.at[p],
            send_sem=c_send.at[i],
            recv_sem=c_recv.at[p],
            device_id=(r, i),
            device_id_type=MESH,
        )

    def one_first(n, c):
        i = (p + 1 + n) % NP

        @pl.when(jnp.logical_not(jnp.logical_and(own, i == p)))
        def _():
            pltpu.make_async_copy(a_land.at[i], a_land.at[i], a_recv.at[i]).wait()

        wide = jnp.dot(a_land[i], spread, preferred_element_type=F32).astype(BF16)
        a_exp[:, :HALF, :] = wide[:, :128].reshape(CAPT, HALF, 128)
        a_exp[:, HALF:, :] = wide[:, 128:].reshape(CAPT, HALF, 128)

        def job(u, c):
            rows, cols = [], []
            for side in range(2):
                code = jobs[side, i, u]
                tile, sel, at = code // 4 % CAPT, code % 4, code // (4 * CAPT)
                x = a_exp[tile].reshape(4, CAPT, 128) * mask[sel][None]
                rows.append(x.reshape(TILE, 128))
                w = ints[at]
                cols += [w * keep[0], w * keep[1]]
            out = jnp.dot(
                jnp.concatenate(rows, axis=1),
                jnp.concatenate(cols, axis=0),
                preferred_element_type=F32,
            )
            top, bottom = out[:HALF], out[HALF:]
            both = jnp.where(
                low, top + pltpu.roll(top, TILE, 1), bottom + pltpu.roll(bottom, TILE, 1)
            )
            parts[i, pl.ds(pl.multiple_of(u * HALF, HALF), HALF), :] = both.astype(BF16)
            return c

        lax.fori_loop(0, LIVE2, job, 0, unroll=4)

        @pl.when(i != p)
        def _():
            parts_copy(i).start()

        return c

    lax.fori_loop(0, NP, one_first, 0)

    total[...] = parts[p].astype(F32).reshape(LIVE2, HALF, 128)

    def add(d, c):
        k = (p + NP - d) % NP
        pltpu.make_async_copy(c_land.at[k], c_land.at[k], c_recv.at[k]).wait()
        total[...] += c_land[k].astype(F32).reshape(LIVE2, HALF, 128)
        return c

    lax.fori_loop(1, NP, add, 0)

    def place(s, c):
        cyc[pl.ds(pl.multiple_of(s * HALF, HALF), HALF), :] = total[slot_of[s]]
        return c

    lax.fori_loop(0, 2 * CAPT, place, 0)
    ovov_copy.wait()
    hist_copy.wait()

    alive = jnp.broadcast_to(live[...], (2 * CAPT, 128))
    col = jnp.concatenate([col_e[...], col_e[...]], axis=1)
    base = pair_e[...] - col
    rows = row_e[...]
    pick_q, pick_lane = iota((TILE, 128), 0), iota((TILE, 128), 1) // TILE

    def finish(m, sums):
        at = pl.ds(pl.multiple_of(m * 128, 128), 128)
        cycle = cyc[pl.ds(m, 2 * CAPT, stride=HALF), :]
        ov = ovov[:, :, at].reshape(2 * CAPT, 128).astype(F32)
        resid = (ov + cycle) * alive
        pick = (pick_q == 2 * m + pick_lane).astype(F32)
        row = jnp.dot(rows, pick, precision=lax.Precision.HIGHEST, preferred_element_type=F32)
        old = amps[:, :, at].reshape(2 * CAPT, 128).astype(F32)
        new = (old + resid / (base - row)) * alive
        new_amps[:, :, at] = new.astype(BF16).reshape(2, CAPT, 128)
        terms = [hist[h, :, :, at].reshape(2 * CAPT, 128).astype(F32) for h in range(NH)]
        terms.append(resid)
        return tuple(
            s + (t * resid).reshape(4, 8, 128).sum(axis=0) for s, t in zip(sums, terms)
        )

    zero = jnp.zeros((8, 128), F32)
    sums = lax.fori_loop(0, HALF, finish, (zero,) * (NH + 1))
    at_row = iota((8, 128), 0)
    mine = zero
    for h, s in enumerate(sums):
        mine = jnp.where(at_row == h, jnp.sum(s, axis=0, keepdims=True), mine)

    def row_copy(d):
        return pltpu.make_async_remote_copy(
            src_ref=g_one.at[r], dst_ref=g_one.at[r], send_sem=g_send.at[d],
            recv_sem=g_recv.at[r], device_id=((r + d) % NR, p), device_id_type=MESH,
        )

    def pair_copy(d):
        return pltpu.make_async_remote_copy(
            src_ref=g_two.at[p], dst_ref=g_two.at[p], send_sem=g_send.at[NR + d],
            recv_sem=g_recv.at[NR + p], device_id=(r, (p + d) % NP), device_id_type=MESH,
        )

    def start_all(copy):
        def step(d, c):
            copy(d).start()
            return c

        return step

    def sent_all(copy):
        def step(d, c):
            copy(d).wait_send()
            return c

        return step

    g_one[r] = mine
    lax.fori_loop(1, NR, start_all(row_copy), 0)

    def got_row(d, c):
        k = (r + NR - d) % NR
        pltpu.make_async_copy(g_one.at[k], g_one.at[k], g_recv.at[k]).wait()
        return c

    lax.fori_loop(1, NR, got_row, 0)
    g_two[p] = jnp.sum(g_one[...], axis=0)
    lax.fori_loop(1, NP, start_all(pair_copy), 0)

    def got_pair(d, c):
        k = (p + NP - d) % NP
        pltpu.make_async_copy(g_two.at[k], g_two.at[k], g_recv.at[NR + k]).wait()
        return c

    lax.fori_loop(1, NP, got_pair, 0)
    everyone = jnp.sum(jnp.sum(g_two[...], axis=0), axis=1, keepdims=True)
    everyone = jnp.broadcast_to(everyone, (8, 128))
    gram[...] = jnp.where(at_row == NH, jnp.sqrt(everyone), everyone) / (TILE * NP)

    lax.fori_loop(1, NR, sent_all(row_copy), 0)
    lax.fori_loop(1, NP, sent_all(pair_copy), 0)

    def sent_parts(d, c):
        parts_copy((p + d) % NP).wait_send()
        return c

    lax.fori_loop(1, NP, sent_parts, 0)

    def sent_amps(n, c):
        @pl.when(to_other(n % 2, n // 2))
        def _():
            amps_copy(n % 2, n // 2).wait_send()

        return c

    lax.fori_loop(0, 2 * NR, sent_amps, 0)


def tables(tile_index, first, second, across):
    dead = across * across
    ns, _, capt = tile_index.shape
    t = jnp.arange(capt, dtype=jnp.int32)
    inner = lax.dynamic_slice(tile_index, (0, first, 0), (ns, 1, capt))
    outer = lax.dynamic_slice(tile_index, (0, second, 0), (ns, 2, capt))
    count = jnp.sum((outer[:, :1] < dead).astype(jnp.int32), axis=2, keepdims=True)
    shift = jnp.concatenate([jnp.zeros_like(count), count], axis=1)
    place = jnp.where(outer < dead, t + shift, -1).reshape(ns, 1, 2 * capt)
    u = jnp.arange(LIVE2, dtype=jnp.int32)[None, :, None]
    packed = jnp.sum(
        jnp.where(place == u, outer.reshape(ns, 1, 2 * capt) - dead, 0), axis=2, keepdims=True
    ) + dead
    which = (u >= count).astype(jnp.int32)
    same = (packed // across == inner // across) & (inner < dead)
    none = dead * capt
    code = (inner % across) * across * capt + t
    lowest = jnp.min(jnp.where(same, t, capt), axis=2, keepdims=True)
    highest = jnp.max(jnp.where(same, t, -1), axis=2, keepdims=True)

    def entry(pick, present):
        found = jnp.sum(jnp.where(t == pick, code, 0), axis=2, keepdims=True)
        found = found + (packed % across) * capt
        return jnp.where(present, found * 4 + which, 2)[..., 0]

    jobs = jnp.stack([entry(lowest, lowest < capt), entry(highest, highest > lowest)])
    return jobs


def local(amps, tile_index, ovov, cycle_ints, history, slab, eps_occ, eps_vir):
    _, jdev, capt, area = amps.shape
    across = cycle_ints.shape[2]
    dead = across * across
    p = lax.axis_index("pair")
    r = lax.axis_index("reorder")
    jobs = tables(tile_index, p, r * jdev, across)
    local_idx = lax.dynamic_slice(tile_index, (p, r * jdev, 0), (1, jdev, capt))[0]
    slots = jnp.arange(capt, dtype=jnp.int32)
    count = jnp.sum((local_idx[0] < dead).astype(jnp.int32))
    slot_of = jnp.concatenate([slots, jnp.minimum(slots + count, LIVE2 - 1)])
    flat = local_idx.reshape(-1)
    live = (flat < dead).astype(F32)[:, None]
    occ = eps_occ[slab]
    pair_e = lax.dynamic_slice(occ, (p,), (1,)) + jnp.repeat(
        lax.dynamic_slice(occ, (r * jdev,), (jdev,)), capt
    )
    vir = eps_vir.reshape(across, TILE)
    row_e = vir[jnp.minimum(flat // across, across - 1)]
    col_e = vir[flat % across]
    ints = cycle_ints[0].transpose(1, 2, 0, 3).reshape(dead, 2, HALF, 128)
    ints = ints.transpose(0, 2, 1, 3).reshape(dead, TILE, 128)

    vmem = pl.BlockSpec(memory_space=pltpu.VMEM)
    smem = pl.BlockSpec(memory_space=pltpu.SMEM)
    hbm = pl.BlockSpec(memory_space=pl.ANY)
    dma = pltpu.SemaphoreType.DMA
    new_amps, gram = pl.pallas_call(
        kernel,
        out_shape=(
            jax.ShapeDtypeStruct((jdev, capt, area), BF16),
            jax.ShapeDtypeStruct((8, 128), F32),
        ),
        in_specs=[smem, smem, vmem, vmem, vmem, vmem, vmem, hbm, hbm, hbm],
        out_specs=(vmem, vmem),
        scratch_shapes=[
            pltpu.VMEM((dead, TILE, 128), BF16),
            pltpu.VMEM((jdev, capt, area), BF16),
            pltpu.VMEM((NH, jdev, capt, area), BF16),
            pltpu.VMEM((2 * capt * HALF, 128), F32),
            pltpu.VMEM((2, capt * HALF, 128), BF16),
            pltpu.VMEM((NP, capt * HALF, 128), BF16),
            pltpu.VMEM((capt, TILE, 128), BF16),
            pltpu.VMEM((3, capt, 128), BF16),
            pltpu.VMEM((NP, LIVE2 * HALF, 128), BF16),
            pltpu.VMEM((NP, LIVE2 * HALF, 128), BF16),
            pltpu.VMEM((LIVE2, HALF, 128), F32),
            pltpu.VMEM((2 * capt * HALF, 128), F32),
            pltpu.VMEM((NR, 8, 128), F32),
            pltpu.VMEM((NP, 8, 128), F32),
            dma((1,)),
            dma((2,)),
            dma((2 * NR,)),
            dma((NP,)),
            dma((NP,)),
            dma((NP,)),
            dma((NR + NP,)),
            dma((NR + NP,)),
        ],
        compiler_params=pltpu.CompilerParams(
            collective_id=0, has_side_effects=True, vmem_limit_bytes=48 << 20
        ),
    )(jobs, slot_of, amps[0], live, pair_e[:, None], row_e, col_e, ovov[0], ints, history[:, 0])
    return new_amps[None], gram[: NH + 1, 0]


def solution(mesh):
    in_specs = (
        P("pair", "reorder", None, None),
        P(),
        P("pair", "reorder", None, None),
        P("pair", "reorder", None, None, None),
        P(None, "pair", "reorder", None, None),
        P(),
        P(),
        P(),
    )
    out_specs = (P("pair", "reorder", None, None), P())
    return jax.shard_map(local, mesh=mesh, in_specs=in_specs, out_specs=out_specs, check_vma=False)
```

```python
import jax
import jax.numpy as jnp
from jax import lax
from jax.experimental import pallas as pl
from jax.experimental.pallas import tpu as pltpu
from jax.sharding import PartitionSpec as P

MESH = pl.DeviceIdType.MESH
TILE = 64
HALF = 32
AREA = TILE * TILE
LIVE2 = 24
NP = 16
NR = 8
CAPT = 16
NH = 6
SIDE = 4
QROWS = CAPT // SIDE * HALF
HROWS = LIVE2 // 2 * HALF
F32, BF16 = jnp.float32, jnp.bfloat16


def iota(shape, dim):
    return lax.broadcasted_iota(jnp.int32, shape, dim)


def kernel(
    jobs, slot_of, amps, live, pair_e, row_e, col_e, ovov_hbm, ints_hbm, hist_hbm,
    new_amps, gram,
    ints, ovov, hist, stage, a_out, z_land, a_land, a_exp, mask, parts, x_land, y_land, x_sum, y_sum,
    x_last, y_last, total, cyc, g_one, g_two,
    w_sem, in_sem, zs_send, zs_recv, xy_send, xy_recv, zg_send, zg_recv, fw_send, fw_recv,
    x_send, x_recv, y_send, y_recv, xl_send, xl_recv, yl_send, yl_recv, g_send, g_recv,
):
    r = lax.axis_index("reorder")
    p = lax.axis_index("pair")
    z, core = r // 2, r % 2
    x, y = p % SIDE, p // SIDE
    main = (p // 2) % 2 == core
    barrier = pltpu.get_barrier_semaphore()

    def remote(src, dst, send, recv, device):
        return pltpu.make_async_remote_copy(
            src_ref=src, dst_ref=dst, send_sem=send, recv_sem=recv, device_id=device, device_id_type=MESH
        )

    def arrive(ref, sem):
        pltpu.make_async_copy(ref, ref, sem).wait()

    w_copy = pltpu.make_async_copy(ints_hbm, ints, w_sem.at[0])
    w_copy.start()
    ovov_copy = pltpu.make_async_copy(ovov_hbm, ovov, in_sem.at[0])
    ovov_copy.start()
    hist_copy = pltpu.make_async_copy(hist_hbm, hist, in_sem.at[1])
    hist_copy.start()

    def greet(device):
        pl.semaphore_signal(barrier, inc=1, device_id=device, device_id_type=MESH)

    for d in range(1, NR):
        greet(((r + d) % NR, p))
    for d in range(1, NP):
        greet((r, (p + d) % NP))

    lane_in, lane_out = iota((128, 128), 0), iota((128, 128), 1)
    half, q = lane_in // TILE, lane_in % TILE
    order = (lane_out == half * TILE + (q % 2) * HALF + q // 2).astype(BF16)

    def turn(m, c):
        v = amps[:, :, pl.ds(pl.multiple_of(m * 128, 128), 128)].reshape(2 * CAPT, 128)
        w = jnp.dot(v, order, preferred_element_type=F32)
        stage[pl.ds(m, 2 * CAPT, stride=HALF), :] = w
        return c

    lax.fori_loop(0, HALF, turn, 0, unroll=8)
    for quarter in range(SIDE):
        for kk in range(2):
            at = (kk * CAPT + quarter * CAPT // SIDE) * HALF
            a_out[quarter, kk] = stage[at : at + QROWS].astype(BF16)

    pl.semaphore_wait(barrier, NR - 1 + NP - 1)

    def scatter(d):
        to = (z + d) % SIDE
        return remote(
            a_out.at[to], z_land.at[z], zs_send.at[d - 1], zs_recv.at[z], (2 * to + core, p)
        )

    for d in range(1, SIDE):
        scatter(d).start()
    z_land[z] = a_out[z]

    def turned(d, kk):
        frm = (z + d) % SIDE
        k = 4 * frm + 2 * core + kk
        return frm, k, remote(
            z_land.at[frm, kk], a_land.at[p, z], xy_send.at[2 * d + kk], xy_recv.at[p], (r, k)
        )

    for d in range(SIDE):
        frm = (z + d) % SIDE
        if d:
            arrive(z_land.at[frm], zs_recv.at[frm])
        for kk in range(2):
            frm, k, copy = turned(d, kk)

            @pl.when(k != p)
            def _():
                copy.start()

            @pl.when(k == p)
            def _():
                a_land[p, z] = z_land[frm, kk]

    def place_of(n):
        d = (n + 1) % NP
        return ((y + d // SIDE) % SIDE) * SIDE + (x + d % SIDE) % SIDE

    def gather(i, e):
        return remote(
            a_land.at[i, z], a_land.at[i, z], zg_send.at[i, e - 1], zg_recv.at[i, z],
            (2 * ((z + e) % SIDE) + core, p),
        )

    @pl.when(main)
    def _():
        def step(n, c):
            i = place_of(n)

            @pl.when(i != p)
            def _():
                arrive(a_land.at[i, z], xy_recv.at[i])

            for e in range(1, SIDE):
                gather(i, e).start()
            return c

        lax.fori_loop(0, NP, step, 0)

    def forward(i):
        return remote(a_land.at[i], a_land.at[i], fw_send.at[i], fw_recv.at[i], (r + 1 - 2 * core, p))

    def collect(n):
        i = place_of(n)

        @pl.when(main)
        def _():
            for e in range(1, SIDE):
                k = (z + e) % SIDE
                arrive(a_land.at[i, k], zg_recv.at[i, k])
            forward(i).start()

    lane_in, lane_out = iota((128, 256), 0), iota((128, 256), 1)
    spread = (lane_in == lane_out // 2).astype(BF16)
    lane = iota((CAPT, 128), 1)
    mask[0] = (lane % 2 == 0).astype(BF16)
    mask[1] = (lane % 2 == 1).astype(BF16)
    mask[2] = jnp.zeros((CAPT, 128), BF16)
    low_f = (iota((TILE, 128), 1) < TILE).astype(F32)
    keep = (low_f.astype(BF16), (1.0 - low_f).astype(BF16))
    low = iota((HALF, 128), 1) < TILE

    w_copy.wait()

    def x_copy(i):
        xi, yi = i % SIDE, i // SIDE
        return remote(
            parts.at[i, pl.ds(0, HROWS)], x_land.at[x, yi], x_send.at[i], x_recv.at[x, yi],
            (r, y * SIDE + xi),
        )

    def y_copy(i):
        xi, yi = i % SIDE, i // SIDE
        return remote(
            parts.at[i, pl.ds(HROWS, HROWS)], y_land.at[y, xi], y_send.at[i], y_recv.at[y, xi],
            (r, yi * SIDE + x),
        )

    def x_total(yi):
        acc = parts[yi * SIDE + x, :HROWS].astype(F32)
        for e in range(1, SIDE):
            k = (x + e) % SIDE
            arrive(x_land.at[k, yi], x_recv.at[k, yi])
            acc += x_land[k, yi].astype(F32)
        return acc

    def y_total(xi):
        acc = parts[y * SIDE + xi, HROWS:].astype(F32)
        for e in range(1, SIDE):
            k = (y + e) % SIDE
            arrive(y_land.at[k, xi], y_recv.at[k, xi])
            acc += y_land[k, xi].astype(F32)
        return acc

    def x_last_copy(e):
        to = (y + e) % SIDE
        return remote(
            x_sum.at[e - 1], x_last.at[y], xl_send.at[e - 1], xl_recv.at[y], (r, to * SIDE + x)
        )

    def y_last_copy(e):
        to = (x + e) % SIDE
        return remote(
            y_sum.at[e - 1], y_last.at[x], yl_send.at[e - 1], yl_recv.at[x], (r, y * SIDE + to)
        )

    def x_pass(e):
        x_sum[e - 1] = x_total((y + e) % SIDE).astype(BF16)
        x_last_copy(e).start()

    def y_pass(e):
        y_sum[e - 1] = y_total((x + e) % SIDE).astype(BF16)
        y_last_copy(e).start()

    collect(0)

    def one_first(n, c):
        i = place_of(n)

        @pl.when(n < NP - 1)
        def _():
            collect(n + 1)

        @pl.when(jnp.logical_not(main))
        def _():
            arrive(a_land.at[i], fw_recv.at[i])

        wide = jnp.dot(
            a_land[i].reshape(CAPT * HALF, 128), spread, preferred_element_type=F32
        ).astype(BF16)
        a_exp[:, :HALF, :] = wide[:, :128].reshape(CAPT, HALF, 128)
        a_exp[:, HALF:, :] = wide[:, 128:].reshape(CAPT, HALF, 128)

        def job(u, c):
            rows, cols = [], []
            for side in range(2):
                code = jobs[side, i, u]
                tile, sel, at = code // 4 % CAPT, code % 4, code // (4 * CAPT)
                v = a_exp[tile].reshape(4, CAPT, 128) * mask[sel][None]
                rows.append(v.reshape(TILE, 128))
                w = ints[at]
                cols += [w * keep[0], w * keep[1]]
            out = jnp.dot(
                jnp.concatenate(rows, axis=1),
                jnp.concatenate(cols, axis=0),
                preferred_element_type=F32,
            )
            top, bottom = out[:HALF], out[HALF:]
            both = jnp.where(
                low, top + pltpu.roll(top, TILE, 1), bottom + pltpu.roll(bottom, TILE, 1)
            )
            parts[i, pl.ds(pl.multiple_of(u * HALF, HALF), HALF), :] = both.astype(BF16)
            return c

        lax.fori_loop(0, LIVE2, job, 0, unroll=LIVE2)

        @pl.when(i % SIDE != x)
        def _():
            x_copy(i).start()

        @pl.when(i // SIDE != y)
        def _():
            y_copy(i).start()

        for e, after in ((1, 8), (2, 12)):

            @pl.when(n == after)
            def _(e=e):
                x_pass(e)

        return c

    lax.fori_loop(0, NP, one_first, 0)
    x_pass(3)
    for e in range(1, SIDE):
        y_pass(e)

    top = x_total(y)
    for e in range(1, SIDE):
        k = (y + e) % SIDE
        arrive(x_last.at[k], xl_recv.at[k])
        top += x_last[k].astype(F32)
    total[: LIVE2 // 2] = top.reshape(LIVE2 // 2, HALF, 128)
    top = y_total(x)
    for e in range(1, SIDE):
        k = (x + e) % SIDE
        arrive(y_last.at[k], yl_recv.at[k])
        top += y_last[k].astype(F32)
    total[LIVE2 // 2 :] = top.reshape(LIVE2 // 2, HALF, 128)

    def place(s, c):
        cyc[pl.ds(pl.multiple_of(s * HALF, HALF), HALF), :] = total[slot_of[s]]
        return c

    lax.fori_loop(0, 2 * CAPT, place, 0, unroll=8)
    ovov_copy.wait()
    hist_copy.wait()

    alive = jnp.broadcast_to(live[...], (2 * CAPT, 128))
    col = jnp.concatenate([col_e[...], col_e[...]], axis=1)
    base = pair_e[...] - col
    rows = row_e[...]
    pick_q, pick_lane = iota((TILE, 128), 0), iota((TILE, 128), 1) // TILE

    def finish(m, sums):
        at = pl.ds(pl.multiple_of(m * 128, 128), 128)
        cycle = cyc[pl.ds(m, 2 * CAPT, stride=HALF), :]
        ov = ovov[:, :, at].reshape(2 * CAPT, 128).astype(F32)
        resid = (ov + cycle) * alive
        pick = (pick_q == 2 * m + pick_lane).astype(F32)
        row = jnp.dot(rows, pick, precision=lax.Precision.HIGHEST, preferred_element_type=F32)
        old = amps[:, :, at].reshape(2 * CAPT, 128).astype(F32)
        new = (old + resid / (base - row)) * alive
        new_amps[:, :, at] = new.astype(BF16).reshape(2, CAPT, 128)
        terms = [hist[h, :, :, at].reshape(2 * CAPT, 128).astype(F32) for h in range(NH)]
        terms.append(resid)
        return tuple(
            s + (t * resid).reshape(4, 8, 128).sum(axis=0) for s, t in zip(sums, terms)
        )

    zero = jnp.zeros((8, 128), F32)
    sums = lax.fori_loop(0, HALF, finish, (zero,) * (NH + 1))
    at_row = iota((8, 128), 0)
    mine = zero
    for h, s in enumerate(sums):
        mine = jnp.where(at_row == h, jnp.sum(s, axis=0, keepdims=True), mine)

    def row_copy(d):
        return remote(
            g_one.at[r], g_one.at[r], g_send.at[d], g_recv.at[r], ((r + d) % NR, p)
        )

    def pair_copy(d):
        return remote(
            g_two.at[p], g_two.at[p], g_send.at[NR + d], g_recv.at[NR + p], (r, (p + d) % NP)
        )

    g_one[r] = mine
    for d in range(1, NR):
        row_copy(d).start()
    for d in range(1, NR):
        k = (r + d) % NR
        arrive(g_one.at[k], g_recv.at[k])
    g_two[p] = jnp.sum(g_one[...], axis=0)
    for d in range(1, NP):
        pair_copy(d).start()
    for d in range(1, NP):
        k = (p + d) % NP
        arrive(g_two.at[k], g_recv.at[NR + k])
    everyone = jnp.sum(jnp.sum(g_two[...], axis=0), axis=1, keepdims=True)
    everyone = jnp.broadcast_to(everyone, (8, 128))
    gram[...] = jnp.where(at_row == NH, jnp.sqrt(everyone), everyone) / (TILE * NP)

    for d in range(1, NR):
        row_copy(d).wait_send()
    for d in range(1, NP):
        pair_copy(d).wait_send()
    for d in range(1, SIDE):
        scatter(d).wait_send()
        x_last_copy(d).wait_send()
        y_last_copy(d).wait_send()
    for d in range(SIDE):
        for kk in range(2):
            frm, k, copy = turned(d, kk)

            @pl.when(k != p)
            def _():
                copy.wait_send()

    def sent(i, c):
        @pl.when(i % SIDE != x)
        def _():
            x_copy(i).wait_send()

        @pl.when(i // SIDE != y)
        def _():
            y_copy(i).wait_send()

        @pl.when(main)
        def _():
            for e in range(1, SIDE):
                gather(i, e).wait_send()
            forward(i).wait_send()

        return c

    lax.fori_loop(0, NP, sent, 0)


def tables(tile_index, first, second, across):
    dead = across * across
    ns, _, capt = tile_index.shape
    t = jnp.arange(capt, dtype=jnp.int32)
    inner = lax.dynamic_slice(tile_index, (0, first, 0), (ns, 1, capt))
    outer = lax.dynamic_slice(tile_index, (0, second, 0), (ns, 2, capt))
    count = jnp.sum((outer[:, :1] < dead).astype(jnp.int32), axis=2, keepdims=True)
    shift = jnp.concatenate([jnp.zeros_like(count), count], axis=1)
    place = jnp.where(outer < dead, t + shift, -1).reshape(ns, 1, 2 * capt)
    u = jnp.arange(LIVE2, dtype=jnp.int32)[None, :, None]
    packed = jnp.sum(
        jnp.where(place == u, outer.reshape(ns, 1, 2 * capt) - dead, 0), axis=2, keepdims=True
    ) + dead
    which = (u >= count).astype(jnp.int32)
    same = (packed // across == inner // across) & (inner < dead)
    none = dead * capt
    code = (inner % across) * across * capt + t
    lowest = jnp.min(jnp.where(same, t, capt), axis=2, keepdims=True)
    highest = jnp.max(jnp.where(same, t, -1), axis=2, keepdims=True)

    def entry(pick, present):
        found = jnp.sum(jnp.where(t == pick, code, 0), axis=2, keepdims=True)
        found = found + (packed % across) * capt
        return jnp.where(present, found * 4 + which, 2)[..., 0]

    jobs = jnp.stack([entry(lowest, lowest < capt), entry(highest, highest > lowest)])
    return jobs


def local(amps, tile_index, ovov, cycle_ints, history, slab, eps_occ, eps_vir):
    _, jdev, capt, area = amps.shape
    across = cycle_ints.shape[2]
    dead = across * across
    p = lax.axis_index("pair")
    r = lax.axis_index("reorder")
    jobs = tables(tile_index, p, r * jdev, across)
    local_idx = lax.dynamic_slice(tile_index, (p, r * jdev, 0), (1, jdev, capt))[0]
    slots = jnp.arange(capt, dtype=jnp.int32)
    count = jnp.sum((local_idx[0] < dead).astype(jnp.int32))
    slot_of = jnp.concatenate([slots, jnp.minimum(slots + count, LIVE2 - 1)])
    flat = local_idx.reshape(-1)
    live = (flat < dead).astype(F32)[:, None]
    occ = eps_occ[slab]
    pair_e = lax.dynamic_slice(occ, (p,), (1,)) + jnp.repeat(
        lax.dynamic_slice(occ, (r * jdev,), (jdev,)), capt
    )
    vir = eps_vir.reshape(across, TILE)
    row_e = vir[jnp.minimum(flat // across, across - 1)]
    col_e = vir[flat % across]
    ints = cycle_ints[0].transpose(1, 2, 0, 3).reshape(dead, 2, HALF, 128)
    ints = ints.transpose(0, 2, 1, 3).reshape(dead, TILE, 128)

    vmem = pl.BlockSpec(memory_space=pltpu.VMEM)
    smem = pl.BlockSpec(memory_space=pltpu.SMEM)
    hbm = pl.BlockSpec(memory_space=pl.ANY)
    dma = pltpu.SemaphoreType.DMA
    new_amps, gram = pl.pallas_call(
        kernel,
        out_shape=(
            jax.ShapeDtypeStruct((jdev, capt, area), BF16),
            jax.ShapeDtypeStruct((8, 128), F32),
        ),
        in_specs=[smem, smem, vmem, vmem, vmem, vmem, vmem, hbm, hbm, hbm],
        out_specs=(vmem, vmem),
        scratch_shapes=[
            pltpu.VMEM((dead, TILE, 128), BF16),
            pltpu.VMEM((jdev, capt, area), BF16),
            pltpu.VMEM((NH, jdev, capt, area), BF16),
            pltpu.VMEM((2 * capt * HALF, 128), F32),
            pltpu.VMEM((SIDE, 2, QROWS, 128), BF16),
            pltpu.VMEM((SIDE, 2, QROWS, 128), BF16),
            pltpu.VMEM((NP, SIDE, QROWS, 128), BF16),
            pltpu.VMEM((capt, TILE, 128), BF16),
            pltpu.VMEM((3, capt, 128), BF16),
            pltpu.VMEM((NP, LIVE2 * HALF, 128), BF16),
            pltpu.VMEM((SIDE, SIDE, HROWS, 128), BF16),
            pltpu.VMEM((SIDE, SIDE, HROWS, 128), BF16),
            pltpu.VMEM((SIDE - 1, HROWS, 128), BF16),
            pltpu.VMEM((SIDE - 1, HROWS, 128), BF16),
            pltpu.VMEM((SIDE, HROWS, 128), BF16),
            pltpu.VMEM((SIDE, HROWS, 128), BF16),
            pltpu.VMEM((LIVE2, HALF, 128), F32),
            pltpu.VMEM((2 * capt * HALF, 128), F32),
            pltpu.VMEM((NR, 8, 128), F32),
            pltpu.VMEM((NP, 8, 128), F32),
            dma((1,)),
            dma((2,)),
            dma((SIDE - 1,)),
            dma((SIDE,)),
            dma((NR,)),
            dma((NP,)),
            dma((NP, SIDE - 1)),
            dma((NP, SIDE)),
            dma((NP,)),
            dma((NP,)),
            dma((NP,)),
            dma((SIDE, SIDE)),
            dma((NP,)),
            dma((SIDE, SIDE)),
            dma((SIDE - 1,)),
            dma((SIDE,)),
            dma((SIDE - 1,)),
            dma((SIDE,)),
            dma((NR + NP,)),
            dma((NR + NP,)),
        ],
        compiler_params=pltpu.CompilerParams(
            collective_id=0, has_side_effects=True, vmem_limit_bytes=48 << 20
        ),
    )(jobs, slot_of, amps[0], live, pair_e[:, None], row_e, col_e, ovov[0], ints, history[:, 0])
    return new_amps[None], gram[: NH + 1, 0]


def solution(mesh):
    in_specs = (
        P("pair", "reorder", None, None),
        P(),
        P("pair", "reorder", None, None),
        P("pair", "reorder", None, None, None),
        P(None, "pair", "reorder", None, None),
        P(),
        P(),
        P(),
    )
    out_specs = (P("pair", "reorder", None, None), P())
    return jax.shard_map(local, mesh=mesh, in_specs=in_specs, out_specs=out_specs, check_vma=False)
```

```python
import jax
import jax.numpy as jnp
from jax import lax
from jax.experimental import pallas as pl
from jax.experimental.pallas import tpu as pltpu
from jax.sharding import PartitionSpec as P

MESH = pl.DeviceIdType.MESH
TILE = 64
HALF = 32
AREA = TILE * TILE
LIVE2 = 24
NP = 16
NR = 8
CAPT = 16
NH = 6
NT = 25
DEAD = NT * NT
SIDE = 4
QROWS = CAPT // SIDE * HALF
HROWS = LIVE2 // 2 * HALF
ORDER = (
    (2, 2), (2, 1), (1, 2), (2, 3), (3, 2), (1, 1), (3, 1), (1, 3), (3, 3),
    (2, 0), (0, 2), (1, 0), (0, 1), (3, 0), (0, 3), (0, 0),
)
F32, BF16 = jnp.float32, jnp.bfloat16


def iota(shape, dim):
    return lax.broadcasted_iota(jnp.int32, shape, dim)


def column(row):
    eye = iota((CAPT, CAPT), 0) == iota((CAPT, CAPT), 1)
    return jnp.sum(jnp.where(eye, row, 0), axis=1, keepdims=True)


def row_col(tile):
    row = (tile * 5243) >> 17
    return row, tile - NT * row


def tables(p, r, tiles, codes):
    t = iota((CAPT, 1), 0)
    u = iota((1, 128), 1)

    def one(i, carry):
        def get(j):
            return column(tiles[i, pl.ds(j, 1), :])

        inner, first, second = get(p), get(2 * r), get(2 * r + 1)
        in_row, in_col = row_col(inner)
        count = jnp.sum((first < DEAD).astype(jnp.int32), axis=0, keepdims=True)
        place = jnp.where(first < DEAD, t, -1)
        place_two = jnp.where(second < DEAD, t + count, -1)
        packed = DEAD + jnp.sum(
            jnp.where(place == u, first - DEAD, 0) + jnp.where(place_two == u, second - DEAD, 0),
            axis=0,
            keepdims=True,
        )
        out_row, out_col = row_col(packed)
        same = jnp.logical_and(in_row == out_row, inner < DEAD)
        lowest = jnp.min(jnp.where(same, t, CAPT), axis=0, keepdims=True)
        highest = jnp.max(jnp.where(same, t, -1), axis=0, keepdims=True)
        base = in_col * (NT * CAPT) + t
        which = jnp.where(u < count, 0, 1)

        def entry(pick, present):
            found = jnp.sum(jnp.where(t == pick, base, 0), axis=0, keepdims=True)
            found = (found + out_col * CAPT) * 4 + which
            return jnp.where(present, found, 2)

        codes[pl.ds(i, 1), :] = entry(lowest, lowest < CAPT)
        codes[pl.ds(NP + i, 1), :] = entry(highest, highest > lowest)
        return carry

    lax.fori_loop(0, NP, one, 0, unroll=4)
    own = tiles[p, pl.ds(2 * r, 1), :]
    count = jnp.sum((own < DEAD).astype(jnp.int32), axis=1, keepdims=True)
    slot = jnp.where(u < CAPT, u, jnp.minimum(u - CAPT + count, LIVE2 - 1))
    codes[2 * NP : 2 * NP + 8, :] = jnp.broadcast_to(slot, (8, 128))


def denominators(p, r, tiles, vir, slab, eps_occ, inverse):
    own = [column(tiles[p, pl.ds(2 * r + j, 1), :]) for j in range(2)]
    tile = jnp.concatenate(own, axis=0)
    alive = jnp.broadcast_to((tile < DEAD).astype(F32), (2 * CAPT, 128))
    row, col = row_col(tile)
    row = jnp.minimum(row, NT - 1)
    lines = [vir[pl.ds(n * 128, 128)].reshape(1, 128) for n in range(NT // 2)]
    last = vir[pl.ds(NT // 2 * 128, TILE)].reshape(1, TILE)
    lines.append(jnp.concatenate([last, last], axis=1))
    lines.append(jnp.zeros((CAPT - len(lines), 128), F32))
    lines = jnp.concatenate(lines, axis=0)
    lane = iota((2 * CAPT, 128), 1)

    def energies(index):
        pair = index >> 1
        pick = (iota((2 * CAPT, CAPT), 1) == pair).astype(F32)
        both = jnp.dot(pick, lines, precision=lax.Precision.HIGHEST, preferred_element_type=F32)
        other = pltpu.roll(both, TILE, 1)
        return jnp.where(lane // TILE == index - 2 * pair, both, other)

    rows, cols = energies(row), energies(col)

    def occ(j):
        return eps_occ[jnp.clip(slab[j], 0, eps_occ.shape[0] - 1)]

    first, second = occ(p), [occ(2 * r + j) for j in range(2)]
    base = jnp.where(iota((2 * CAPT, 128), 0) < CAPT, first + second[0], first + second[1]) - cols
    pick_q, pick_lane = iota((128, 128), 0), iota((128, 128), 1) // TILE

    def one(m, c):
        pick = (pick_q == 2 * m + pick_lane).astype(F32)
        row = jnp.dot(rows, pick, precision=lax.Precision.HIGHEST, preferred_element_type=F32)
        at = pl.ds(pl.multiple_of(m * 2 * CAPT, 2 * CAPT), 2 * CAPT)
        inverse[at, :] = alive / (base - row)
        return c

    lax.fori_loop(0, HALF, one, 0, unroll=4)
    return alive


def kernel(
    slab, eps_occ, amps_hbm, tiles_hbm, ovov_hbm, ints_hbm, hist_hbm, vir_hbm,
    new_amps, gram,
    amps, tiles, vir, codes, jobs, inverse, ints, ovov, hist, stage, a_out, z_land, a_land, a_exp, mask, parts, x_land, y_land, x_sum, y_sum,
    x_last, y_last, total, cyc, g_one, g_two,
    in_sem, code_sem, zs_send, zs_recv, xy_send, xy_recv, zg_send, zg_recv, fw_send, fw_recv,
    x_send, x_recv, y_send, y_recv, xl_send, xl_recv, yl_send, yl_recv, g_send, g_recv,
):
    r = lax.axis_index("reorder")
    p = lax.axis_index("pair")
    z, core = r // 2, r % 2
    x, y = p % SIDE, p // SIDE
    main = (p // 2) % 2 == core
    barrier = pltpu.get_barrier_semaphore()

    def remote(src, dst, send, recv, device):
        return pltpu.make_async_remote_copy(
            src_ref=src, dst_ref=dst, send_sem=send, recv_sem=recv, device_id=device, device_id_type=MESH
        )

    def arrive(ref, sem):
        pltpu.make_async_copy(ref, ref, sem).wait()

    loads = [
        pltpu.make_async_copy(src, dst, in_sem.at[n])
        for n, (src, dst) in enumerate(
            ((amps_hbm, amps), (tiles_hbm, tiles), (vir_hbm, vir), (ints_hbm, ints), (ovov_hbm, ovov), (hist_hbm, hist))
        )
    ]
    for load in loads:
        load.start()
    amps_copy, tiles_copy, vir_copy, w_copy, ovov_copy, hist_copy = loads

    def greet(device):
        pl.semaphore_signal(barrier, inc=1, device_id=device, device_id_type=MESH)

    for d in range(1, NR):
        greet(((r + d) % NR, p))
    for d in range(1, NP):
        greet((r, (p + d) % NP))

    lane_in, lane_out = iota((128, 128), 0), iota((128, 128), 1)
    half, q = lane_in // TILE, lane_in % TILE
    order = (lane_out == half * TILE + (q % 2) * HALF + q // 2).astype(BF16)

    def turn(m, c):
        v = amps[:, :, pl.ds(pl.multiple_of(m * 128, 128), 128)].reshape(2 * CAPT, 128)
        w = jnp.dot(v, order, preferred_element_type=F32)
        stage[pl.ds(m, 2 * CAPT, stride=HALF), :] = w
        return c

    amps_copy.wait()
    lax.fori_loop(0, HALF, turn, 0, unroll=8)
    for quarter in range(SIDE):
        for kk in range(2):
            at = (kk * CAPT + quarter * CAPT // SIDE) * HALF
            a_out[quarter, kk] = stage[at : at + QROWS].astype(BF16)

    pl.semaphore_wait(barrier, NR - 1 + NP - 1)

    def scatter(d):
        to = (z + d) % SIDE
        return remote(
            a_out.at[to], z_land.at[z], zs_send.at[d - 1], zs_recv.at[z], (2 * to + core, p)
        )

    for d in range(1, SIDE):
        scatter(d).start()
    z_land[z] = a_out[z]

    tiles_copy.wait()
    vir_copy.wait()
    tables(p, r, tiles, codes)
    code_copy = pltpu.make_async_copy(codes, jobs, code_sem.at[0])
    code_copy.start()
    alive = denominators(p, r, tiles, vir, slab, eps_occ, inverse)

    def turned(d, kk):
        frm = (z + d) % SIDE
        k = 4 * frm + 2 * core + kk
        return frm, k, remote(
            z_land.at[frm, kk], a_land.at[p, z], xy_send.at[2 * d + kk], xy_recv.at[p], (r, k)
        )

    for d in range(SIDE):
        frm = (z + d) % SIDE
        if d:
            arrive(z_land.at[frm], zs_recv.at[frm])
        for kk in range(2):
            frm, k, copy = turned(d, kk)

            @pl.when(k != p)
            def _():
                copy.start()

            @pl.when(k == p)
            def _():
                a_land[p, z] = z_land[frm, kk]

    def place_of(n):
        d = 0
        for at, (dx, dy) in enumerate(ORDER):
            d = jnp.where(n == at, dy * SIDE + dx, d)
        return ((y + d // SIDE) % SIDE) * SIDE + (x + d % SIDE) % SIDE

    def gather(i, e):
        return remote(
            a_land.at[i, z], a_land.at[i, z], zg_send.at[i, e - 1], zg_recv.at[i, z],
            (2 * ((z + e) % SIDE) + core, p),
        )

    @pl.when(main)
    def _():
        def step(n, c):
            i = place_of(n)

            @pl.when(i != p)
            def _():
                arrive(a_land.at[i, z], xy_recv.at[i])

            for e in range(1, SIDE):
                gather(i, e).start()
            return c

        lax.fori_loop(0, NP, step, 0)

    def forward(i):
        return remote(a_land.at[i], a_land.at[i], fw_send.at[i], fw_recv.at[i], (r + 1 - 2 * core, p))

    def collect(n):
        i = place_of(n)

        @pl.when(main)
        def _():
            for e in range(1, SIDE):
                k = (z + e) % SIDE
                arrive(a_land.at[i, k], zg_recv.at[i, k])
            forward(i).start()

    lane_in, lane_out = iota((128, 256), 0), iota((128, 256), 1)
    spread = (lane_in == lane_out // 2).astype(BF16)
    lane = iota((CAPT, 128), 1)
    mask[0] = (lane % 2 == 0).astype(BF16)
    mask[1] = (lane % 2 == 1).astype(BF16)
    mask[2] = jnp.zeros((CAPT, 128), BF16)
    low_f = (iota((TILE, 128), 1) < TILE).astype(F32)
    keep = (low_f.astype(BF16), (1.0 - low_f).astype(BF16))
    low = iota((HALF, 128), 1) < TILE

    w_copy.wait()
    code_copy.wait()

    def x_copy(i):
        xi, yi = i % SIDE, i // SIDE
        return remote(
            parts.at[i, pl.ds(0, HROWS)], x_land.at[x, yi], x_send.at[i], x_recv.at[x, yi],
            (r, y * SIDE + xi),
        )

    def y_copy(i):
        xi, yi = i % SIDE, i // SIDE
        return remote(
            parts.at[i, pl.ds(HROWS, HROWS)], y_land.at[y, xi], y_send.at[i], y_recv.at[y, xi],
            (r, yi * SIDE + x),
        )

    def x_total(yi):
        acc = parts[yi * SIDE + x, :HROWS].astype(F32)
        for e in range(1, SIDE):
            k = (x + e) % SIDE
            arrive(x_land.at[k, yi], x_recv.at[k, yi])
            acc += x_land[k, yi].astype(F32)
        return acc

    def y_total(xi):
        acc = parts[y * SIDE + xi, HROWS:].astype(F32)
        for e in range(1, SIDE):
            k = (y + e) % SIDE
            arrive(y_land.at[k, xi], y_recv.at[k, xi])
            acc += y_land[k, xi].astype(F32)
        return acc

    def x_last_copy(e):
        to = (y + e) % SIDE
        return remote(
            x_sum.at[e - 1], x_last.at[y], xl_send.at[e - 1], xl_recv.at[y], (r, to * SIDE + x)
        )

    def y_last_copy(e):
        to = (x + e) % SIDE
        return remote(
            y_sum.at[e - 1], y_last.at[x], yl_send.at[e - 1], yl_recv.at[x], (r, y * SIDE + to)
        )

    def x_pass(e):
        x_sum[e - 1] = x_total((y + e) % SIDE).astype(BF16)
        x_last_copy(e).start()

    def y_pass(e):
        y_sum[e - 1] = y_total((x + e) % SIDE).astype(BF16)
        y_last_copy(e).start()

    collect(0)

    def one_first(n, c):
        i = place_of(n)

        @pl.when(n < NP - 1)
        def _():
            collect(n + 1)

        @pl.when(jnp.logical_not(main))
        def _():
            arrive(a_land.at[i], fw_recv.at[i])

        wide = jnp.dot(
            a_land[i].reshape(CAPT * HALF, 128), spread, preferred_element_type=F32
        ).astype(BF16)
        a_exp[:, :HALF, :] = wide[:, :128].reshape(CAPT, HALF, 128)
        a_exp[:, HALF:, :] = wide[:, 128:].reshape(CAPT, HALF, 128)

        def job(u, c):
            rows, cols = [], []
            for side in range(2):
                code = jobs[side * NP + i, u]
                tile, sel, at = (code >> 2) & (CAPT - 1), code & 3, code >> 6
                sel, at = jnp.minimum(sel, 2), jnp.clip(at, 0, DEAD - 1)
                v = a_exp[tile].reshape(4, CAPT, 128) * mask[sel][None]
                rows.append(v.reshape(TILE, 128))
                w = ints[at]
                cols += [w * keep[0], w * keep[1]]
            out = jnp.dot(
                jnp.concatenate(rows, axis=1),
                jnp.concatenate(cols, axis=0),
                preferred_element_type=F32,
            )
            top, bottom = out[:HALF], out[HALF:]
            both = jnp.where(
                low, top + pltpu.roll(top, TILE, 1), bottom + pltpu.roll(bottom, TILE, 1)
            )
            parts[i, pl.ds(pl.multiple_of(u * HALF, HALF), HALF), :] = both.astype(BF16)
            return c

        lax.fori_loop(0, LIVE2, job, 0, unroll=LIVE2)

        @pl.when(i % SIDE != x)
        def _():
            x_copy(i).start()

        @pl.when(i // SIDE != y)
        def _():
            y_copy(i).start()

        for e in range(1, SIDE):

            @pl.when(n == ORDER.index((e, 0)))
            def _(e=e):
                y_pass(e)

            @pl.when(n == ORDER.index((0, e)))
            def _(e=e):
                x_pass(e)

        return c

    lax.fori_loop(0, NP, one_first, 0)

    top = x_total(y)
    for e in range(1, SIDE):
        k = (y + e) % SIDE
        arrive(x_last.at[k], xl_recv.at[k])
        top += x_last[k].astype(F32)
    total[: LIVE2 // 2] = top.reshape(LIVE2 // 2, HALF, 128)
    top = y_total(x)
    for e in range(1, SIDE):
        k = (x + e) % SIDE
        arrive(y_last.at[k], yl_recv.at[k])
        top += y_last[k].astype(F32)
    total[LIVE2 // 2 :] = top.reshape(LIVE2 // 2, HALF, 128)

    def place(s, c):
        cyc[pl.ds(pl.multiple_of(s * HALF, HALF), HALF), :] = total[jnp.clip(jobs[2 * NP, s], 0, LIVE2 - 1)]
        return c

    lax.fori_loop(0, 2 * CAPT, place, 0, unroll=8)
    ovov_copy.wait()
    hist_copy.wait()

    def correlate(m, sums):
        at = pl.ds(pl.multiple_of(m * 128, 128), 128)
        cycle = cyc[pl.ds(m, 2 * CAPT, stride=HALF), :]
        ov = ovov[:, :, at].reshape(2 * CAPT, 128).astype(F32)
        resid = (ov + cycle) * alive
        stage[pl.ds(pl.multiple_of(m * 2 * CAPT, 2 * CAPT), 2 * CAPT), :] = resid
        terms = [hist[h, :, :, at].reshape(2 * CAPT, 128).astype(F32) for h in range(NH)]
        terms.append(resid)
        return tuple(
            s + (t * resid).reshape(4, 8, 128).sum(axis=0) for s, t in zip(sums, terms)
        )

    zero = jnp.zeros((8, 128), F32)
    sums = lax.fori_loop(0, HALF, correlate, (zero,) * (NH + 1), unroll=4)
    at_row = iota((8, 128), 0)
    mine = zero
    for h, s in enumerate(sums):
        mine = jnp.where(at_row == h, jnp.sum(s, axis=0, keepdims=True), mine)

    def row_copy(d):
        return remote(
            g_one.at[r], g_one.at[r], g_send.at[d], g_recv.at[r], ((r + d) % NR, p)
        )

    def pair_copy(d):
        return remote(
            g_two.at[p], g_two.at[p], g_send.at[NR + d], g_recv.at[NR + p], (r, (p + d) % NP)
        )

    g_one[r] = mine
    for d in range(1, NR):
        row_copy(d).start()

    def update(m, c):
        at = pl.ds(pl.multiple_of(m * 128, 128), 128)
        rows = pl.ds(pl.multiple_of(m * 2 * CAPT, 2 * CAPT), 2 * CAPT)
        old = amps[:, :, at].reshape(2 * CAPT, 128).astype(F32)
        new = old * alive + stage[rows, :] * inverse[rows, :]
        new_amps[:, :, at] = new.astype(BF16).reshape(2, CAPT, 128)
        return c

    lax.fori_loop(0, HALF, update, 0, unroll=8)
    for d in range(1, NR):
        k = (r + d) % NR
        arrive(g_one.at[k], g_recv.at[k])
    g_two[p] = jnp.sum(g_one[...], axis=0)
    for d in range(1, NP):
        pair_copy(d).start()
    for d in range(1, NP):
        k = (p + d) % NP
        arrive(g_two.at[k], g_recv.at[NR + k])
    everyone = jnp.sum(jnp.sum(g_two[...], axis=0), axis=1, keepdims=True)
    everyone = jnp.broadcast_to(everyone, (8, 128))
    gram[...] = jnp.where(at_row == NH, jnp.sqrt(everyone), everyone) / (TILE * NP)

    for d in range(1, NR):
        row_copy(d).wait_send()
    for d in range(1, NP):
        pair_copy(d).wait_send()
    for d in range(1, SIDE):
        scatter(d).wait_send()
        x_last_copy(d).wait_send()
        y_last_copy(d).wait_send()
    for d in range(SIDE):
        for kk in range(2):
            frm, k, copy = turned(d, kk)

            @pl.when(k != p)
            def _():
                copy.wait_send()

    def sent(i, c):
        @pl.when(i % SIDE != x)
        def _():
            x_copy(i).wait_send()

        @pl.when(i // SIDE != y)
        def _():
            y_copy(i).wait_send()

        @pl.when(main)
        def _():
            for e in range(1, SIDE):
                gather(i, e).wait_send()
            forward(i).wait_send()

        return c

    lax.fori_loop(0, NP, sent, 0)


def local(amps, tile_index, ovov, cycle_ints, history, slab, eps_occ, eps_vir):
    _, jdev, capt, area = amps.shape
    across = cycle_ints.shape[2]
    dead = across * across
    ints = cycle_ints[0].transpose(1, 2, 0, 3).reshape(dead, 2, HALF, 128)
    ints = ints.transpose(0, 2, 1, 3).reshape(dead, TILE, 128)

    vmem = pl.BlockSpec(memory_space=pltpu.VMEM)
    smem = pl.BlockSpec(memory_space=pltpu.SMEM)
    hbm = pl.BlockSpec(memory_space=pltpu.HBM)
    dma = pltpu.SemaphoreType.DMA
    new_amps, gram = pl.pallas_call(
        kernel,
        out_shape=(
            jax.ShapeDtypeStruct((jdev, capt, area), BF16),
            jax.ShapeDtypeStruct((8, 128), F32),
        ),
        in_specs=[smem, smem] + [hbm] * 6,
        out_specs=(vmem, vmem),
        scratch_shapes=[
            pltpu.VMEM((jdev, capt, area), BF16),
            pltpu.VMEM(tile_index.shape, jnp.int32),
            pltpu.VMEM(eps_vir.shape, F32),
            pltpu.VMEM((2 * NP + 8, 128), jnp.int32),
            pltpu.SMEM((2 * NP + 8, 128), jnp.int32),
            pltpu.VMEM((2 * capt * HALF, 128), F32),
            pltpu.VMEM((dead, TILE, 128), BF16),
            pltpu.VMEM((jdev, capt, area), BF16),
            pltpu.VMEM((NH, jdev, capt, area), BF16),
            pltpu.VMEM((2 * capt * HALF, 128), F32),
            pltpu.VMEM((SIDE, 2, QROWS, 128), BF16),
            pltpu.VMEM((SIDE, 2, QROWS, 128), BF16),
            pltpu.VMEM((NP, SIDE, QROWS, 128), BF16),
            pltpu.VMEM((capt, TILE, 128), BF16),
            pltpu.VMEM((3, capt, 128), BF16),
            pltpu.VMEM((NP, LIVE2 * HALF, 128), BF16),
            pltpu.VMEM((SIDE, SIDE, HROWS, 128), BF16),
            pltpu.VMEM((SIDE, SIDE, HROWS, 128), BF16),
            pltpu.VMEM((SIDE - 1, HROWS, 128), BF16),
            pltpu.VMEM((SIDE - 1, HROWS, 128), BF16),
            pltpu.VMEM((SIDE, HROWS, 128), BF16),
            pltpu.VMEM((SIDE, HROWS, 128), BF16),
            pltpu.VMEM((LIVE2, HALF, 128), F32),
            pltpu.VMEM((2 * capt * HALF, 128), F32),
            pltpu.VMEM((NR, 8, 128), F32),
            pltpu.VMEM((NP, 8, 128), F32),
            dma((6,)),
            dma((1,)),
            dma((SIDE - 1,)),
            dma((SIDE,)),
            dma((NR,)),
            dma((NP,)),
            dma((NP, SIDE - 1)),
            dma((NP, SIDE)),
            dma((NP,)),
            dma((NP,)),
            dma((NP,)),
            dma((SIDE, SIDE)),
            dma((NP,)),
            dma((SIDE, SIDE)),
            dma((SIDE - 1,)),
            dma((SIDE,)),
            dma((SIDE - 1,)),
            dma((SIDE,)),
            dma((NR + NP,)),
            dma((NR + NP,)),
        ],
        compiler_params=pltpu.CompilerParams(
            collective_id=0, has_side_effects=True, vmem_limit_bytes=48 << 20
        ),
    )(slab, eps_occ, amps[0], tile_index, ovov[0], ints, history[:, 0], eps_vir)
    return new_amps[None], gram[: NH + 1, 0]


def solution(mesh):
    in_specs = (
        P("pair", "reorder", None, None),
        P(),
        P("pair", "reorder", None, None),
        P("pair", "reorder", None, None, None),
        P(None, "pair", "reorder", None, None),
        P(),
        P(),
        P(),
    )
    out_specs = (P("pair", "reorder", None, None), P())
    return jax.shard_map(local, mesh=mesh, in_specs=in_specs, out_specs=out_specs, check_vma=False)
```

```python
import jax
import jax.numpy as jnp
from jax import lax
from jax.experimental import pallas as pl
from jax.experimental.pallas import tpu as pltpu
from jax.sharding import PartitionSpec as P

MESH = pl.DeviceIdType.MESH
TILE = 64
HALF = 32
AREA = TILE * TILE
LIVE2 = 24
NP = 16
NR = 8
CAPT = 16
NH = 6
NT = 25
DEAD = NT * NT
SIDE = 4
QROWS = CAPT // SIDE * HALF
HROWS = LIVE2 // 2 * HALF
AHEAD = 4
RROWS = HROWS // 2
ROWS = (2, 1, 3, 0)
ORDER = (
    (2, 2), (2, 1), (1, 2), (2, 3), (3, 2), (1, 1), (3, 1), (1, 3),
    (3, 3), (2, 0), (0, 2), (1, 0), (0, 1), (3, 0), (0, 3), (0, 0),
)
F32, BF16 = jnp.float32, jnp.bfloat16


def iota(shape, dim):
    return lax.broadcasted_iota(jnp.int32, shape, dim)


def column(row):
    eye = iota((CAPT, CAPT), 0) == iota((CAPT, CAPT), 1)
    return jnp.sum(jnp.where(eye, row, 0), axis=1, keepdims=True)


def row_col(tile):
    row = (tile * 5243) >> 17
    return row, tile - NT * row


def tables(p, r, tiles, codes):
    t = iota((CAPT, 1), 0)
    u = iota((1, 128), 1)

    def one(i, carry):
        def get(j):
            return column(tiles[i, pl.ds(j, 1), :])

        inner, first, second = get(p), get(2 * r), get(2 * r + 1)
        in_row, in_col = row_col(inner)
        count = jnp.sum((first < DEAD).astype(jnp.int32), axis=0, keepdims=True)
        place = jnp.where(first < DEAD, t, -1)
        place_two = jnp.where(second < DEAD, t + count, -1)
        packed = DEAD + jnp.sum(
            jnp.where(place == u, first - DEAD, 0) + jnp.where(place_two == u, second - DEAD, 0),
            axis=0,
            keepdims=True,
        )
        out_row, out_col = row_col(packed)
        same = jnp.logical_and(in_row == out_row, inner < DEAD)
        lowest = jnp.min(jnp.where(same, t, CAPT), axis=0, keepdims=True)
        highest = jnp.max(jnp.where(same, t, -1), axis=0, keepdims=True)
        base = in_col * (NT * CAPT) + t
        which = jnp.where(u < count, 0, 1)

        def entry(pick, present):
            found = jnp.sum(jnp.where(t == pick, base, 0), axis=0, keepdims=True)
            found = (found + out_col * CAPT) * 4 + which
            return jnp.where(present, found, 2)

        codes[pl.ds(i, 1), :] = entry(lowest, lowest < CAPT)
        codes[pl.ds(NP + i, 1), :] = entry(highest, highest > lowest)
        return carry

    lax.fori_loop(0, NP, one, 0, unroll=4)
    own = tiles[p, pl.ds(2 * r, 1), :]
    count = jnp.sum((own < DEAD).astype(jnp.int32), axis=1, keepdims=True)
    slot = jnp.where(u < CAPT, u, jnp.minimum(u - CAPT + count, LIVE2 - 1))
    codes[2 * NP : 2 * NP + 8, :] = jnp.broadcast_to(slot, (8, 128))


def denominators(p, r, tiles, vir, slab, eps_occ, inverse):
    own = [column(tiles[p, pl.ds(2 * r + j, 1), :]) for j in range(2)]
    tile = jnp.concatenate(own, axis=0)
    alive = jnp.broadcast_to((tile < DEAD).astype(F32), (2 * CAPT, 128))
    row, col = row_col(tile)
    row = jnp.minimum(row, NT - 1)
    lines = [vir[pl.ds(n * 128, 128)].reshape(1, 128) for n in range(NT // 2)]
    last = vir[pl.ds(NT // 2 * 128, TILE)].reshape(1, TILE)
    lines.append(jnp.concatenate([last, last], axis=1))
    lines.append(jnp.zeros((CAPT - len(lines), 128), F32))
    lines = jnp.concatenate(lines, axis=0)
    lane = iota((2 * CAPT, 128), 1)

    def energies(index):
        pair = index >> 1
        pick = (iota((2 * CAPT, CAPT), 1) == pair).astype(F32)
        both = jnp.dot(pick, lines, precision=lax.Precision.HIGHEST, preferred_element_type=F32)
        other = pltpu.roll(both, TILE, 1)
        return jnp.where(lane // TILE == index - 2 * pair, both, other)

    rows, cols = energies(row), energies(col)

    def occ(j):
        return eps_occ[jnp.clip(slab[j], 0, eps_occ.shape[0] - 1)]

    first, second = occ(p), [occ(2 * r + j) for j in range(2)]
    base = jnp.where(iota((2 * CAPT, 128), 0) < CAPT, first + second[0], first + second[1]) - cols
    pick_q, pick_lane = iota((128, 128), 0), iota((128, 128), 1) // TILE

    def one(m, c):
        pick = (pick_q == 2 * m + pick_lane).astype(F32)
        row = jnp.dot(rows, pick, precision=lax.Precision.HIGHEST, preferred_element_type=F32)
        at = pl.ds(pl.multiple_of(m * 2 * CAPT, 2 * CAPT), 2 * CAPT)
        inverse[at, :] = alive / (base - row)
        return c

    lax.fori_loop(0, HALF, one, 0, unroll=4)
    return alive


def kernel(
    slab_hbm, occ_hbm, amps_hbm, tiles_hbm, ovov_hbm, ints_hbm, hist_hbm, vir_hbm,
    new_amps, gram,
    slab, eps_occ, amps, tiles, vir, codes, jobs, inverse, ints, ovov, hist, stage, a_out, z_land, a_land, a_exp, mask, parts, x_relay, y_relay, x_land, y_land, x_sum, y_sum,
    x_last, y_last, total, cyc, g_one, g_two,
    in_sem, code_sem, zs_send, zs_recv, xy_send, xy_recv, zg_send, zg_recv, fw_send, fw_recv,
    xr_send, xr_recv, yr_send, yr_recv, x_send, x_recv, y_send, y_recv, xl_send, xl_recv, yl_send, yl_recv, g_send, g_recv,
):
    r = lax.axis_index("reorder")
    p = lax.axis_index("pair")
    z, core = r // 2, r % 2
    x, y = p % SIDE, p // SIDE
    main = (p // 2) % 2 == core
    barrier = pltpu.get_barrier_semaphore()

    def remote(src, dst, send, recv, device):
        return pltpu.make_async_remote_copy(
            src_ref=src, dst_ref=dst, send_sem=send, recv_sem=recv, device_id=device, device_id_type=MESH
        )

    def arrive(ref, sem):
        pltpu.make_async_copy(ref, ref, sem).wait()

    loads = [
        pltpu.make_async_copy(src, dst, in_sem.at[n])
        for n, (src, dst) in enumerate(
            (
                (amps_hbm, amps), (tiles_hbm, tiles), (vir_hbm, vir), (slab_hbm, slab), (occ_hbm, eps_occ),
                (ints_hbm, ints), (ovov_hbm, ovov), (hist_hbm, hist),
            )
        )
    ]
    for load in loads:
        load.start()
    amps_copy, tiles_copy, vir_copy, slab_copy, occ_copy, w_copy, ovov_copy, hist_copy = loads

    def greet(device):
        pl.semaphore_signal(barrier, inc=1, device_id=device, device_id_type=MESH)

    for d in range(1, NR):
        greet(((r + d) % NR, p))
    for d in range(1, NP):
        greet((r, (p + d) % NP))

    lane_in, lane_out = iota((128, 128), 0), iota((128, 128), 1)
    half, q = lane_in // TILE, lane_in % TILE
    order = (lane_out == half * TILE + (q % 2) * HALF + q // 2).astype(BF16)

    def turn(m, c):
        v = amps[:, :, pl.ds(pl.multiple_of(m * 128, 128), 128)].reshape(2 * CAPT, 128)
        w = jnp.dot(v, order, preferred_element_type=F32)
        stage[pl.ds(m, 2 * CAPT, stride=HALF), :] = w
        return c

    amps_copy.wait()
    lax.fori_loop(0, HALF, turn, 0, unroll=8)
    for quarter in range(SIDE):
        for kk in range(2):
            at = (kk * CAPT + quarter * CAPT // SIDE) * HALF
            a_out[quarter, kk] = stage[at : at + QROWS].astype(BF16)

    tiles_copy.wait()
    vir_copy.wait()
    slab_copy.wait()
    occ_copy.wait()
    tables(p, r, tiles, codes)
    code_copy = pltpu.make_async_copy(codes, jobs, code_sem.at[0])
    code_copy.start()
    alive = denominators(p, r, tiles, vir, slab, eps_occ, inverse)

    pl.semaphore_wait(barrier, NR - 1 + NP - 1)

    def scatter(d):
        to = (z + d) % SIDE
        return remote(
            a_out.at[to], z_land.at[z], zs_send.at[d - 1], zs_recv.at[z], (2 * to + core, p)
        )

    for d in range(1, SIDE):
        scatter(d).start()
    z_land[z] = a_out[z]

    def turned(dy, kk):
        frm = (y + SIDE - dy) % SIDE
        k = 4 * frm + 2 * core + kk
        return frm, k, remote(
            z_land.at[frm, kk], a_land.at[p, z], xy_send.at[2 * dy + kk], xy_recv.at[p], (r, k)
        )

    for dy in ROWS:
        frm = (y + SIDE - dy) % SIDE

        @pl.when(frm != z)
        def _():
            arrive(z_land.at[frm], zs_recv.at[frm])

        for kk in range(2):
            frm, k, copy = turned(dy, kk)

            @pl.when(k != p)
            def _():
                copy.start()

            @pl.when(k == p)
            def _():
                a_land[p, z] = z_land[frm, kk]

    def place_of(n):
        d = 0
        for at, (dx, dy) in enumerate(ORDER):
            d = jnp.where(n == at, dy * SIDE + dx, d)
        return ((y + d // SIDE) % SIDE) * SIDE + (x + d % SIDE) % SIDE

    def gather(i, e):
        return remote(
            a_land.at[i, z], a_land.at[i, z], zg_send.at[i, e - 1], zg_recv.at[i, z],
            (2 * ((z + e) % SIDE) + core, p),
        )

    def spread_planes(n):
        i = place_of(n)

        @pl.when(main)
        def _():
            @pl.when(i != p)
            def _():
                arrive(a_land.at[i, z], xy_recv.at[i])

            for e in (2, 1, 3):
                gather(i, e).start()

    for n in range(AHEAD):
        spread_planes(n)

    def forward(i):
        return remote(a_land.at[i], a_land.at[i], fw_send.at[i], fw_recv.at[i], (r + 1 - 2 * core, p))

    def collect(n):
        i = place_of(n)

        @pl.when(main)
        def _():
            for e in range(1, SIDE):
                k = (z + e) % SIDE
                arrive(a_land.at[i, k], zg_recv.at[i, k])
            forward(i).start()

    lane_in, lane_out = iota((128, 256), 0), iota((128, 256), 1)
    spread = (lane_in == lane_out // 2).astype(BF16)
    lane = iota((CAPT, 128), 1)
    mask[0] = (lane % 2 == 0).astype(BF16)
    mask[1] = (lane % 2 == 1).astype(BF16)
    mask[2] = jnp.zeros((CAPT, 128), BF16)
    low_f = (iota((TILE, 128), 1) < TILE).astype(F32)
    keep = (low_f.astype(BF16), (1.0 - low_f).astype(BF16))
    low = iota((HALF, 128), 1) < TILE

    w_copy.wait()
    code_copy.wait()

    def x_copy(i):
        xi, yi = i % SIDE, i // SIDE
        return remote(
            parts.at[i, pl.ds(0, HROWS)], x_land.at[x, yi], x_send.at[i], x_recv.at[x, yi],
            (r, y * SIDE + xi),
        )

    def y_copy(i):
        xi, yi = i % SIDE, i // SIDE
        return remote(
            parts.at[i, pl.ds(HROWS, HROWS)], y_land.at[y, xi], y_send.at[i], y_recv.at[y, xi],
            (r, yi * SIDE + x),
        )

    def x_total(yi):
        acc = parts[yi * SIDE + x, :HROWS].astype(F32)
        for e in range(1, SIDE):
            k = (x + e) % SIDE
            arrive(x_land.at[k, yi], x_recv.at[k, yi])
            acc += x_land[k, yi].astype(F32)
        return acc

    def y_total(xi):
        acc = parts[y * SIDE + xi, HROWS:].astype(F32)
        for e in range(1, SIDE):
            k = (y + e) % SIDE
            arrive(y_land.at[k, xi], y_recv.at[k, xi])
            acc += y_land[k, xi].astype(F32)
        return acc

    def x_last_copy(e):
        to = (y + e) % SIDE
        return remote(
            x_sum.at[e - 1], x_last.at[y], xl_send.at[e - 1], xl_recv.at[y], (r, to * SIDE + x)
        )

    def y_last_copy(e):
        to = (x + e) % SIDE
        return remote(
            y_sum.at[e - 1], y_last.at[x], yl_send.at[e - 1], yl_recv.at[x], (r, y * SIDE + to)
        )

    def x_pass(e):
        x_sum[e - 1] = x_total((y + e) % SIDE).astype(BF16)
        x_last_copy(e).start()

    def y_pass(e):
        y_sum[e - 1] = y_total((x + e) % SIDE).astype(BF16)
        y_last_copy(e).start()

    collect(0)

    def one_first(n, c):
        i = place_of(n)

        @pl.when(n < NP - 1)
        def _():
            collect(n + 1)

        @pl.when(n < NP - AHEAD)
        def _():
            spread_planes(n + AHEAD)

        @pl.when(jnp.logical_not(main))
        def _():
            arrive(a_land.at[i], fw_recv.at[i])

        wide = jnp.dot(
            a_land[i].reshape(CAPT * HALF, 128), spread, preferred_element_type=F32
        ).astype(BF16)
        a_exp[:, :HALF, :] = wide[:, :128].reshape(CAPT, HALF, 128)
        a_exp[:, HALF:, :] = wide[:, 128:].reshape(CAPT, HALF, 128)

        def job(u, c):
            rows, cols = [], []
            for side in range(2):
                code = jobs[side * NP + i, u]
                tile, sel, at = (code >> 2) & (CAPT - 1), code & 3, code >> 6
                sel, at = jnp.minimum(sel, 2), jnp.clip(at, 0, DEAD - 1)
                v = a_exp[tile].reshape(4, CAPT, 128) * mask[sel][None]
                rows.append(v.reshape(TILE, 128))
                w = ints[at]
                cols += [w * keep[0], w * keep[1]]
            out = jnp.dot(
                jnp.concatenate(rows, axis=1),
                jnp.concatenate(cols, axis=0),
                preferred_element_type=F32,
            )
            top, bottom = out[:HALF], out[HALF:]
            both = jnp.where(
                low, top + pltpu.roll(top, TILE, 1), bottom + pltpu.roll(bottom, TILE, 1)
            )
            parts[i, pl.ds(pl.multiple_of(u * HALF, HALF), HALF), :] = both.astype(BF16)
            return c

        lax.fori_loop(0, LIVE2, job, 0, unroll=LIVE2)

        @pl.when(i % SIDE != x)
        def _():
            x_copy(i).start()

        @pl.when(i // SIDE != y)
        def _():
            y_copy(i).start()

        for e in range(1, SIDE):

            @pl.when(n == {1: 11, 2: 9, 3: 13}[e])
            def _(e=e):
                y_pass(e)

            @pl.when(n == {1: 12, 2: 10, 3: 14}[e])
            def _(e=e):
                x_pass(e)

        return c

    lax.fori_loop(0, NP, one_first, 0)

    top = x_total(y)
    for e in range(1, SIDE):
        k = (y + e) % SIDE
        arrive(x_last.at[k], xl_recv.at[k])
        top += x_last[k].astype(F32)
    total[: LIVE2 // 2] = top.reshape(LIVE2 // 2, HALF, 128)
    top = y_total(x)
    for e in range(1, SIDE):
        k = (x + e) % SIDE
        arrive(y_last.at[k], yl_recv.at[k])
        top += y_last[k].astype(F32)
    total[LIVE2 // 2 :] = top.reshape(LIVE2 // 2, HALF, 128)

    def place(s, c):
        cyc[pl.ds(pl.multiple_of(s * HALF, HALF), HALF), :] = total[jnp.clip(jobs[2 * NP, s], 0, LIVE2 - 1)]
        return c

    lax.fori_loop(0, 2 * CAPT, place, 0, unroll=8)
    ovov_copy.wait()
    hist_copy.wait()

    def correlate(m, sums):
        at = pl.ds(pl.multiple_of(m * 128, 128), 128)
        cycle = cyc[pl.ds(m, 2 * CAPT, stride=HALF), :]
        ov = ovov[:, :, at].reshape(2 * CAPT, 128).astype(F32)
        resid = (ov + cycle) * alive
        stage[pl.ds(pl.multiple_of(m * 2 * CAPT, 2 * CAPT), 2 * CAPT), :] = resid
        terms = [hist[h, :, :, at].reshape(2 * CAPT, 128).astype(F32) for h in range(NH)]
        terms.append(resid)
        return tuple(
            s + (t * resid).reshape(4, 8, 128).sum(axis=0) for s, t in zip(sums, terms)
        )

    zero = jnp.zeros((8, 128), F32)
    sums = lax.fori_loop(0, HALF, correlate, (zero,) * (NH + 1), unroll=4)
    at_lane = iota((1, 128), 1)
    mine = jnp.zeros((1, 128), F32)
    for h, s in enumerate(sums):
        s = jnp.sum(jnp.sum(s, axis=0, keepdims=True), axis=1, keepdims=True)
        mine = jnp.where(at_lane == h, s, mine)

    def row_copy(d):
        return remote(
            g_one.at[r], g_one.at[r], g_send.at[d], g_recv.at[r], ((r + d) % NR, p)
        )

    def pair_copy(d):
        return remote(
            g_two.at[p], g_two.at[p], g_send.at[NR + d], g_recv.at[NR + p], (r, (p + d) % NP)
        )

    g_one[r] = mine
    for d in range(1, NR):
        row_copy(d).start()

    def update(m, c):
        at = pl.ds(pl.multiple_of(m * 128, 128), 128)
        rows = pl.ds(pl.multiple_of(m * 2 * CAPT, 2 * CAPT), 2 * CAPT)
        old = amps[:, :, at].reshape(2 * CAPT, 128).astype(F32)
        new = old * alive + stage[rows, :] * inverse[rows, :]
        new_amps[:, :, at] = new.astype(BF16).reshape(2, CAPT, 128)
        return c

    lax.fori_loop(0, HALF, update, 0, unroll=8)

    for d in range(1, SIDE):
        scatter(d).wait_send()
        x_last_copy(d).wait_send()
        y_last_copy(d).wait_send()
    for d in range(SIDE):
        for kk in range(2):
            frm, k, copy = turned(d, kk)

            @pl.when(k != p)
            def _():
                copy.wait_send()

    def sent(i, c):
        @pl.when(i % SIDE != x)
        def _():
            x_copy(i).wait_send()

        @pl.when(i // SIDE != y)
        def _():
            y_copy(i).wait_send()

        @pl.when(main)
        def _():
            for e in range(1, SIDE):
                gather(i, e).wait_send()
            forward(i).wait_send()

        return c

    lax.fori_loop(0, NP, sent, 0)

    for d in range(1, NR):
        k = (r + d) % NR
        arrive(g_one.at[k], g_recv.at[k])
    g_two[p] = jnp.sum(g_one[...], axis=0)
    for d in range(1, NP):
        pair_copy(d).start()
    for d in range(1, NP):
        k = (p + d) % NP
        arrive(g_two.at[k], g_recv.at[NR + k])
    everyone = jnp.sum(g_two[...], axis=0)
    gram[...] = jnp.where(at_lane == NH, jnp.sqrt(everyone), everyone) / (TILE * NP)

    for d in range(1, NR):
        row_copy(d).wait_send()
    for d in range(1, NP):
        pair_copy(d).wait_send()


def local(amps, tile_index, ovov, cycle_ints, history, slab, eps_occ, eps_vir):
    _, jdev, capt, area = amps.shape
    across = cycle_ints.shape[2]
    dead = across * across
    ints = cycle_ints[0].transpose(1, 2, 0, 3).reshape(dead, 2, HALF, 128)
    ints = ints.transpose(0, 2, 1, 3).reshape(dead, TILE, 128)

    vmem = pl.BlockSpec(memory_space=pltpu.VMEM)
    hbm = pl.BlockSpec(memory_space=pltpu.HBM)
    dma = pltpu.SemaphoreType.DMA
    new_amps, gram = pl.pallas_call(
        kernel,
        out_shape=(
            jax.ShapeDtypeStruct((jdev, capt, area), BF16),
            jax.ShapeDtypeStruct((1, 128), F32),
        ),
        in_specs=[hbm] * 8,
        out_specs=(vmem, vmem),
        scratch_shapes=[
            pltpu.SMEM(slab.shape, jnp.int32),
            pltpu.SMEM(eps_occ.shape, F32),
            pltpu.VMEM((jdev, capt, area), BF16),
            pltpu.VMEM(tile_index.shape, jnp.int32),
            pltpu.VMEM(eps_vir.shape, F32),
            pltpu.VMEM((2 * NP + 8, 128), jnp.int32),
            pltpu.SMEM((2 * NP + 8, 128), jnp.int32),
            pltpu.VMEM((2 * capt * HALF, 128), F32),
            pltpu.VMEM((dead, TILE, 128), BF16),
            pltpu.VMEM((jdev, capt, area), BF16),
            pltpu.VMEM((NH, jdev, capt, area), BF16),
            pltpu.VMEM((2 * capt * HALF, 128), F32),
            pltpu.VMEM((SIDE, 2, QROWS, 128), BF16),
            pltpu.VMEM((SIDE, 2, QROWS, 128), BF16),
            pltpu.VMEM((NP, SIDE, QROWS, 128), BF16),
            pltpu.VMEM((capt, TILE, 128), BF16),
            pltpu.VMEM((3, capt, 128), BF16),
            pltpu.VMEM((NP, LIVE2 * HALF, 128), BF16),
            pltpu.VMEM((2, SIDE, RROWS, 128), BF16),
            pltpu.VMEM((2, SIDE, RROWS, 128), BF16),
            pltpu.VMEM((SIDE, SIDE, HROWS, 128), BF16),
            pltpu.VMEM((SIDE, SIDE, HROWS, 128), BF16),
            pltpu.VMEM((SIDE - 1, HROWS, 128), BF16),
            pltpu.VMEM((SIDE - 1, HROWS, 128), BF16),
            pltpu.VMEM((SIDE, HROWS, 128), BF16),
            pltpu.VMEM((SIDE, HROWS, 128), BF16),
            pltpu.VMEM((LIVE2, HALF, 128), F32),
            pltpu.VMEM((2 * capt * HALF, 128), F32),
            pltpu.VMEM((NR, 1, 128), F32),
            pltpu.VMEM((NP, 1, 128), F32),
            dma((8,)),
            dma((1,)),
            dma((SIDE - 1,)),
            dma((SIDE,)),
            dma((NR,)),
            dma((NP,)),
            dma((NP, SIDE - 1)),
            dma((NP, SIDE)),
            dma((NP,)),
            dma((NP,)),
            dma((2, SIDE)),
            dma((2, SIDE)),
            dma((2, SIDE)),
            dma((2, SIDE)),
            dma((NP,)),
            dma((SIDE, SIDE)),
            dma((NP,)),
            dma((SIDE, SIDE)),
            dma((SIDE - 1,)),
            dma((SIDE,)),
            dma((SIDE - 1,)),
            dma((SIDE,)),
            dma((NR + NP,)),
            dma((NR + NP,)),
        ],
        compiler_params=pltpu.CompilerParams(
            collective_id=0, has_side_effects=True, vmem_limit_bytes=60 << 20
        ),
    )(slab, eps_occ, amps[0], tile_index, ovov[0], ints, history[:, 0], eps_vir)
    return new_amps[None], gram[0, : NH + 1]


def solution(mesh):
    in_specs = (
        P("pair", "reorder", None, None),
        P(),
        P("pair", "reorder", None, None),
        P("pair", "reorder", None, None, None),
        P(None, "pair", "reorder", None, None),
        P(),
        P(),
        P(),
    )
    out_specs = (P("pair", "reorder", None, None), P())
    return jax.shard_map(local, mesh=mesh, in_specs=in_specs, out_specs=out_specs, check_vma=False)
```

```python
import jax
import jax.numpy as jnp
from jax import lax
from jax.experimental import pallas as pl
from jax.experimental.pallas import tpu as pltpu
from jax.sharding import PartitionSpec as P

MESH = pl.DeviceIdType.MESH
TILE = 64
HALF = 32
AREA = TILE * TILE
LIVE2 = 24
NP = 16
NR = 8
CAPT = 16
NH = 6
NT = 25
DEAD = NT * NT
SIDE = 4
QROWS = CAPT // SIDE * HALF
HROWS = LIVE2 // 2 * HALF
AHEAD = 6
RROWS = HROWS // 2
ROWS = (2, 1, 3, 0)
ORDER = (
    (2, 2), (2, 1), (1, 2), (2, 3), (3, 2), (2, 0), (0, 2), (1, 1),
    (3, 3), (1, 3), (3, 1), (1, 0), (0, 1), (3, 0), (0, 3), (0, 0),
)
LAG, FIRST_SHARE = 3, 7
Y_PASS = {2: 10, 1: 13, 3: 14}
X_PASS = {2: 11, 1: 14, 3: 15}
F32, BF16 = jnp.float32, jnp.bfloat16


def iota(shape, dim):
    return lax.broadcasted_iota(jnp.int32, shape, dim)


def column(row):
    eye = iota((CAPT, CAPT), 0) == iota((CAPT, CAPT), 1)
    return jnp.sum(jnp.where(eye, row, 0), axis=1, keepdims=True)


def row_col(tile):
    row = (tile * 5243) >> 17
    return row, tile - NT * row


def tables(p, r, tiles, codes):
    t = iota((CAPT, 1), 0)
    u = iota((1, 128), 1)

    def one(i, carry):
        def get(j):
            return column(tiles[i, pl.ds(j, 1), :])

        inner, first, second = get(p), get(2 * r), get(2 * r + 1)
        in_row, in_col = row_col(inner)
        count = jnp.sum((first < DEAD).astype(jnp.int32), axis=0, keepdims=True)
        place = jnp.where(first < DEAD, t, -1)
        place_two = jnp.where(second < DEAD, t + count, -1)
        packed = DEAD + jnp.sum(
            jnp.where(place == u, first - DEAD, 0) + jnp.where(place_two == u, second - DEAD, 0),
            axis=0,
            keepdims=True,
        )
        out_row, out_col = row_col(packed)
        same = jnp.logical_and(in_row == out_row, inner < DEAD)
        lowest = jnp.min(jnp.where(same, t, CAPT), axis=0, keepdims=True)
        highest = jnp.max(jnp.where(same, t, -1), axis=0, keepdims=True)
        base = in_col * (NT * CAPT) + t
        which = jnp.where(u < count, 0, 1)

        def entry(pick, present):
            found = jnp.sum(jnp.where(t == pick, base, 0), axis=0, keepdims=True)
            found = (found + out_col * CAPT) * 4 + which
            return jnp.where(present, found, 2)

        codes[pl.ds(i, 1), :] = entry(lowest, lowest < CAPT)
        codes[pl.ds(NP + i, 1), :] = entry(highest, highest > lowest)
        return carry

    lax.fori_loop(0, NP, one, 0, unroll=4)
    own = tiles[p, pl.ds(2 * r, 1), :]
    count = jnp.sum((own < DEAD).astype(jnp.int32), axis=1, keepdims=True)
    slot = jnp.where(u < CAPT, u, jnp.minimum(u - CAPT + count, LIVE2 - 1))
    codes[2 * NP : 2 * NP + 8, :] = jnp.broadcast_to(slot, (8, 128))


def denominators(p, r, tiles, vir, slab, eps_occ, inverse):
    own = [column(tiles[p, pl.ds(2 * r + j, 1), :]) for j in range(2)]
    tile = jnp.concatenate(own, axis=0)
    alive = jnp.broadcast_to((tile < DEAD).astype(F32), (2 * CAPT, 128))
    row, col = row_col(tile)
    row = jnp.minimum(row, NT - 1)
    lines = [vir[pl.ds(n * 128, 128)].reshape(1, 128) for n in range(NT // 2)]
    last = vir[pl.ds(NT // 2 * 128, TILE)].reshape(1, TILE)
    lines.append(jnp.concatenate([last, last], axis=1))
    lines.append(jnp.zeros((CAPT - len(lines), 128), F32))
    lines = jnp.concatenate(lines, axis=0)
    lane = iota((2 * CAPT, 128), 1)

    def energies(index):
        pair = index >> 1
        pick = (iota((2 * CAPT, CAPT), 1) == pair).astype(F32)
        both = jnp.dot(pick, lines, precision=lax.Precision.HIGHEST, preferred_element_type=F32)
        other = pltpu.roll(both, TILE, 1)
        return jnp.where(lane // TILE == index - 2 * pair, both, other)

    rows, cols = energies(row), energies(col)

    def occ(j):
        return eps_occ[jnp.clip(slab[j], 0, eps_occ.shape[0] - 1)]

    first, second = occ(p), [occ(2 * r + j) for j in range(2)]
    base = jnp.where(iota((2 * CAPT, 128), 0) < CAPT, first + second[0], first + second[1]) - cols
    pick_q, pick_lane = iota((128, 128), 0), iota((128, 128), 1) // TILE

    def one(m, c):
        pick = (pick_q == 2 * m + pick_lane).astype(F32)
        row = jnp.dot(rows, pick, precision=lax.Precision.HIGHEST, preferred_element_type=F32)
        at = pl.ds(pl.multiple_of(m * 2 * CAPT, 2 * CAPT), 2 * CAPT)
        inverse[at, :] = alive / (base - row)
        return c

    lax.fori_loop(0, HALF, one, 0, unroll=4)
    return alive


def kernel(
    slab_hbm, occ_hbm, amps_hbm, tiles_hbm, ovov_hbm, ints_hbm, hist_hbm, vir_hbm,
    new_amps, gram,
    slab, eps_occ, amps, tiles, vir, codes, jobs, inverse, ints, ovov, hist, stage, a_out, z_land, a_land, a_exp, mask, parts, x_relay, y_relay, x_land, y_land, x_sum, y_sum,
    x_last, y_last, total, cyc, g_one, g_two,
    in_sem, code_sem, zs_send, zs_recv, xy_send, xy_recv, zg_send, zg_recv, fw_send, fw_recv,
    xr_send, xr_recv, yr_send, yr_recv, x_send, x_recv, y_send, y_recv, xl_send, xl_recv, yl_send, yl_recv, g_send, g_recv,
):
    r = lax.axis_index("reorder")
    p = lax.axis_index("pair")
    z, core = r // 2, r % 2
    x, y = p % SIDE, p // SIDE
    main = (p // 2) % 2 == core
    barrier = pltpu.get_barrier_semaphore()

    def remote(src, dst, send, recv, device):
        return pltpu.make_async_remote_copy(
            src_ref=src, dst_ref=dst, send_sem=send, recv_sem=recv, device_id=device, device_id_type=MESH
        )

    def arrive(ref, sem):
        pltpu.make_async_copy(ref, ref, sem).wait()

    loads = [
        pltpu.make_async_copy(src, dst, in_sem.at[n])
        for n, (src, dst) in enumerate(
            (
                (amps_hbm, amps), (tiles_hbm, tiles), (vir_hbm, vir), (slab_hbm, slab), (occ_hbm, eps_occ),
                (ints_hbm, ints), (ovov_hbm, ovov), (hist_hbm, hist),
            )
        )
    ]
    for load in loads:
        load.start()
    amps_copy, tiles_copy, vir_copy, slab_copy, occ_copy, w_copy, ovov_copy, hist_copy = loads

    def greet(device):
        pl.semaphore_signal(barrier, inc=1, device_id=device, device_id_type=MESH)

    for d in range(1, NR):
        greet(((r + d) % NR, p))
    for d in range(1, NP):
        greet((r, (p + d) % NP))

    lane_in, lane_out = iota((128, 128), 0), iota((128, 128), 1)
    half, q = lane_in // TILE, lane_in % TILE
    order = (lane_out == half * TILE + (q % 2) * HALF + q // 2).astype(BF16)

    def turn(m, c):
        v = amps[:, :, pl.ds(pl.multiple_of(m * 128, 128), 128)].reshape(2 * CAPT, 128)
        w = jnp.dot(v, order, preferred_element_type=F32)
        stage[pl.ds(m, 2 * CAPT, stride=HALF), :] = w
        return c

    amps_copy.wait()
    lax.fori_loop(0, HALF, turn, 0, unroll=8)
    for quarter in range(SIDE):
        for kk in range(2):
            at = (kk * CAPT + quarter * CAPT // SIDE) * HALF
            a_out[quarter, kk] = stage[at : at + QROWS].astype(BF16)

    tiles_copy.wait()
    vir_copy.wait()
    slab_copy.wait()
    occ_copy.wait()
    tables(p, r, tiles, codes)
    code_copy = pltpu.make_async_copy(codes, jobs, code_sem.at[0])
    code_copy.start()
    alive = denominators(p, r, tiles, vir, slab, eps_occ, inverse)

    pl.semaphore_wait(barrier, NR - 1 + NP - 1)

    def scatter(d):
        to = (z + d) % SIDE
        return remote(
            a_out.at[to], z_land.at[z], zs_send.at[d - 1], zs_recv.at[z], (2 * to + core, p)
        )

    for d in range(1, SIDE):
        scatter(d).start()
    z_land[z] = a_out[z]

    def turned(dy, kk):
        frm = (y + SIDE - dy) % SIDE
        k = 4 * frm + 2 * core + kk
        return frm, k, remote(
            z_land.at[frm, kk], a_land.at[p, z], xy_send.at[2 * dy + kk], xy_recv.at[p], (r, k)
        )

    for dy in ROWS:
        frm = (y + SIDE - dy) % SIDE

        @pl.when(frm != z)
        def _():
            arrive(z_land.at[frm], zs_recv.at[frm])

        for kk in range(2):
            frm, k, copy = turned(dy, kk)

            @pl.when(k != p)
            def _():
                copy.start()

            @pl.when(k == p)
            def _():
                a_land[p, z] = z_land[frm, kk]

    def place_of(n):
        d = 0
        for at, (dx, dy) in enumerate(ORDER):
            d = jnp.where(n == at, dy * SIDE + dx, d)
        return ((y + d // SIDE) % SIDE) * SIDE + (x + d % SIDE) % SIDE

    def gather(i, e):
        return remote(
            a_land.at[i, z], a_land.at[i, z], zg_send.at[i, e - 1], zg_recv.at[i, z],
            (2 * ((z + e) % SIDE) + core, p),
        )

    def spread_planes(n):
        i = place_of(n)

        @pl.when(main)
        def _():
            @pl.when(i != p)
            def _():
                arrive(a_land.at[i, z], xy_recv.at[i])

            for e in (2, 1, 3):
                gather(i, e).start()

    for n in range(AHEAD):
        spread_planes(n)

    def forward(i):
        return remote(a_land.at[i], a_land.at[i], fw_send.at[i], fw_recv.at[i], (r + 1 - 2 * core, p))

    def collect(n):
        i = place_of(n)

        @pl.when(main)
        def _():
            for e in range(1, SIDE):
                k = (z + e) % SIDE
                arrive(a_land.at[i, k], zg_recv.at[i, k])
            forward(i).start()

    lane_in, lane_out = iota((128, 256), 0), iota((128, 256), 1)
    spread = (lane_in == lane_out // 2).astype(BF16)
    lane = iota((CAPT, 128), 1)
    mask[0] = (lane % 2 == 0).astype(BF16)
    mask[1] = (lane % 2 == 1).astype(BF16)
    mask[2] = jnp.zeros((CAPT, 128), BF16)
    low_f = (iota((TILE, 128), 1) < TILE).astype(F32)
    keep = (low_f.astype(BF16), (1.0 - low_f).astype(BF16))
    low = iota((HALF, 128), 1) < TILE
    low_b = iota((TILE, 128), 1) < TILE
    none = jnp.zeros((TILE, 128), BF16)

    w_copy.wait()
    code_copy.wait()

    def device(dx, dy):
        return (r, (y + dy) % SIDE * SIDE + (x + dx) % SIDE)

    def relay(i, side, along_x):
        first = (0 if along_x else HROWS) + side * RROWS
        xi, yi = i % SIDE, i // SIDE
        line = yi if along_x else xi
        land, send, recv = (x_relay, xr_send, xr_recv) if along_x else (y_relay, yr_send, yr_recv)
        step = 1 - 2 * side
        return remote(
            parts.at[i, pl.ds(first, RROWS)], land.at[side, line], send.at[side, line], recv.at[side, line],
            device(step, 0) if along_x else device(0, step),
        )

    def share(i, side, along_x):
        xi, yi = i % SIDE, i // SIDE
        line = yi if along_x else xi
        land, send, recv = (x_land, x_send, x_recv) if along_x else (y_land, y_send, y_recv)
        step = 1 - 2 * side
        return remote(
            parts.at[i, pl.ds(0 if along_x else HROWS, HROWS)], land.at[side, line], send.at[side, line],
            recv.at[side, line], device(step, 0) if along_x else device(0, step),
        )

    def send_relays(i, along_x):
        away = (i % SIDE - x if along_x else i // SIDE - y) % SIDE

        @pl.when(away == 2)
        def _():
            for side in range(2):
                relay(i, side, along_x).start()

    def send_share(i, along_x):
        away = (i % SIDE - x if along_x else i // SIDE - y) % SIDE
        line = i // SIDE if along_x else i % SIDE
        land, recv = (x_relay, xr_recv) if along_x else (y_relay, yr_recv)

        for side in range(2):

            @pl.when(away == 1 + 2 * side)
            def _(side=side):
                arrive(land.at[side, line], recv.at[side, line])
                first = (0 if along_x else HROWS) + side * RROWS
                own = parts[i, first : first + RROWS].astype(F32)
                parts[i, first : first + RROWS] = (own + land[side, line].astype(F32)).astype(BF16)
                share(i, side, along_x).start()

    def delivered(i, along_x):
        away = (i % SIDE - x if along_x else i // SIDE - y) % SIDE

        @pl.when(away == 2)
        def _():
            for side in range(2):
                relay(i, side, along_x).wait_send()

        for side in range(2):

            @pl.when(away == 1 + 2 * side)
            def _(side=side):
                share(i, side, along_x).wait_send()

    def x_total(yi):
        acc = parts[yi * SIDE + x, :HROWS].astype(F32)
        for side in range(2):
            arrive(x_land.at[side, yi], x_recv.at[side, yi])
            acc += x_land[side, yi].astype(F32)
        return acc

    def y_total(xi):
        acc = parts[y * SIDE + xi, HROWS:].astype(F32)
        for side in range(2):
            arrive(y_land.at[side, xi], y_recv.at[side, xi])
            acc += y_land[side, xi].astype(F32)
        return acc

    def x_last_copy(e):
        to = (y + e) % SIDE
        return remote(
            x_sum.at[e - 1], x_last.at[y], xl_send.at[e - 1], xl_recv.at[y], (r, to * SIDE + x)
        )

    def y_last_copy(e):
        to = (x + e) % SIDE
        return remote(
            y_sum.at[e - 1], y_last.at[x], yl_send.at[e - 1], yl_recv.at[x], (r, y * SIDE + to)
        )

    def x_pass(e):
        x_sum[e - 1] = x_total((y + e) % SIDE).astype(BF16)
        x_last_copy(e).start()

    def y_pass(e):
        y_sum[e - 1] = y_total((x + e) % SIDE).astype(BF16)
        y_last_copy(e).start()

    collect(0)
    collect(1)

    def one_first(n, c):
        i = place_of(n)

        @pl.when(n < NP - 2)
        def _():
            collect(n + 2)

        @pl.when(n < NP - AHEAD)
        def _():
            spread_planes(n + AHEAD)

        @pl.when(jnp.logical_not(main))
        def _():
            arrive(a_land.at[i], fw_recv.at[i])

        wide = jnp.dot(
            a_land[i].reshape(CAPT * HALF, 128), spread, preferred_element_type=F32
        ).astype(BF16)
        a_exp[:, :HALF, :] = wide[:, :128].reshape(CAPT, HALF, 128)
        a_exp[:, HALF:, :] = wide[:, 128:].reshape(CAPT, HALF, 128)

        def job(u, c):
            rows, cols = [], []
            for side in range(2):
                code = jobs[side * NP + i, u]
                tile, sel, at = (code >> 2) & (CAPT - 1), code & 3, code >> 6
                sel, at = jnp.minimum(sel, 2), jnp.clip(at, 0, DEAD - 1)
                v = a_exp[tile].reshape(4, CAPT, 128) * mask[sel][None]
                rows.append(v.reshape(TILE, 128))
                w = ints[at]
                cols += [jnp.where(low_b, w, none), jnp.where(low_b, none, w)]
            out = jnp.dot(
                jnp.concatenate(rows, axis=1),
                jnp.concatenate(cols, axis=0),
                preferred_element_type=F32,
            )
            top, bottom = out[:HALF], out[HALF:]
            both = jnp.where(
                low, top + pltpu.roll(top, TILE, 1), bottom + pltpu.roll(bottom, TILE, 1)
            )
            parts[i, pl.ds(pl.multiple_of(u * HALF, HALF), HALF), :] = both.astype(BF16)
            return c

        lax.fori_loop(0, LIVE2, job, 0, unroll=LIVE2)

        send_relays(i, True)
        send_relays(i, False)

        @pl.when(jnp.logical_and(n >= FIRST_SHARE - LAG, n <= FIRST_SHARE))
        def _():
            late = place_of(n - LAG)
            send_share(late, True)
            send_share(late, False)

        @pl.when(n >= FIRST_SHARE)
        def _():
            send_share(i, True)
            send_share(i, False)

        for e in range(1, SIDE):

            @pl.when(n == Y_PASS[e])
            def _(e=e):
                y_pass(e)

            @pl.when(n == X_PASS[e])
            def _(e=e):
                x_pass(e)

        return c

    lax.fori_loop(0, NP, one_first, 0)

    top = x_total(y)
    for e in range(1, SIDE):
        k = (y + e) % SIDE
        arrive(x_last.at[k], xl_recv.at[k])
        top += x_last[k].astype(F32)
    total[: LIVE2 // 2] = top.reshape(LIVE2 // 2, HALF, 128)
    top = y_total(x)
    for e in range(1, SIDE):
        k = (x + e) % SIDE
        arrive(y_last.at[k], yl_recv.at[k])
        top += y_last[k].astype(F32)
    total[LIVE2 // 2 :] = top.reshape(LIVE2 // 2, HALF, 128)

    def place(s, c):
        cyc[pl.ds(pl.multiple_of(s * HALF, HALF), HALF), :] = total[jnp.clip(jobs[2 * NP, s], 0, LIVE2 - 1)]
        return c

    lax.fori_loop(0, 2 * CAPT, place, 0, unroll=8)
    ovov_copy.wait()
    hist_copy.wait()

    def correlate(m, sums):
        at = pl.ds(pl.multiple_of(m * 128, 128), 128)
        cycle = cyc[pl.ds(m, 2 * CAPT, stride=HALF), :]
        ov = ovov[:, :, at].reshape(2 * CAPT, 128).astype(F32)
        resid = (ov + cycle) * alive
        stage[pl.ds(pl.multiple_of(m * 2 * CAPT, 2 * CAPT), 2 * CAPT), :] = resid
        terms = [hist[h, :, :, at].reshape(2 * CAPT, 128).astype(F32) for h in range(NH)]
        terms.append(resid)
        return tuple(
            s + (t * resid).reshape(4, 8, 128).sum(axis=0) for s, t in zip(sums, terms)
        )

    zero = jnp.zeros((8, 128), F32)
    sums = lax.fori_loop(0, HALF, correlate, (zero,) * (NH + 1), unroll=4)
    at_lane = iota((1, 128), 1)
    mine = jnp.zeros((1, 128), F32)
    for h, s in enumerate(sums):
        s = jnp.sum(jnp.sum(s, axis=0, keepdims=True), axis=1, keepdims=True)
        mine = jnp.where(at_lane == h, s, mine)

    def row_copy(d):
        return remote(
            g_one.at[r], g_one.at[r], g_send.at[d], g_recv.at[r], ((r + d) % NR, p)
        )

    def pair_copy(d):
        return remote(
            g_two.at[p], g_two.at[p], g_send.at[NR + d], g_recv.at[NR + p], (r, (p + d) % NP)
        )

    g_one[r] = mine
    for d in range(1, NR):
        row_copy(d).start()

    def update(m, c):
        at = pl.ds(pl.multiple_of(m * 128, 128), 128)
        rows = pl.ds(pl.multiple_of(m * 2 * CAPT, 2 * CAPT), 2 * CAPT)
        old = amps[:, :, at].reshape(2 * CAPT, 128).astype(F32)
        new = old * alive + stage[rows, :] * inverse[rows, :]
        new_amps[:, :, at] = new.astype(BF16).reshape(2, CAPT, 128)
        return c

    lax.fori_loop(0, HALF, update, 0, unroll=8)

    for d in range(1, SIDE):
        scatter(d).wait_send()
        x_last_copy(d).wait_send()
        y_last_copy(d).wait_send()
    for d in range(SIDE):
        for kk in range(2):
            frm, k, copy = turned(d, kk)

            @pl.when(k != p)
            def _():
                copy.wait_send()

    def sent(i, c):
        delivered(i, True)
        delivered(i, False)

        @pl.when(main)
        def _():
            for e in range(1, SIDE):
                gather(i, e).wait_send()
            forward(i).wait_send()

        return c

    lax.fori_loop(0, NP, sent, 0)

    for d in range(1, NR):
        k = (r + d) % NR
        arrive(g_one.at[k], g_recv.at[k])
    g_two[p] = jnp.sum(g_one[...], axis=0)
    for d in range(1, NP):
        pair_copy(d).start()
    for d in range(1, NP):
        k = (p + d) % NP
        arrive(g_two.at[k], g_recv.at[NR + k])
    everyone = jnp.sum(g_two[...], axis=0)
    gram[...] = jnp.where(at_lane == NH, jnp.sqrt(everyone), everyone) / (TILE * NP)

    for d in range(1, NR):
        row_copy(d).wait_send()
    for d in range(1, NP):
        pair_copy(d).wait_send()


def local(amps, tile_index, ovov, cycle_ints, history, slab, eps_occ, eps_vir):
    _, jdev, capt, area = amps.shape
    across = cycle_ints.shape[2]
    dead = across * across
    ints = cycle_ints[0].transpose(1, 2, 0, 3).reshape(dead, 2, HALF, 128)
    ints = ints.transpose(0, 2, 1, 3).reshape(dead, TILE, 128)

    vmem = pl.BlockSpec(memory_space=pltpu.VMEM)
    hbm = pl.BlockSpec(memory_space=pltpu.HBM)
    dma = pltpu.SemaphoreType.DMA
    new_amps, gram = pl.pallas_call(
        kernel,
        out_shape=(
            jax.ShapeDtypeStruct((jdev, capt, area), BF16),
            jax.ShapeDtypeStruct((1, 128), F32),
        ),
        in_specs=[hbm] * 8,
        out_specs=(vmem, vmem),
        scratch_shapes=[
            pltpu.SMEM(slab.shape, jnp.int32),
            pltpu.SMEM(eps_occ.shape, F32),
            pltpu.VMEM((jdev, capt, area), BF16),
            pltpu.VMEM(tile_index.shape, jnp.int32),
            pltpu.VMEM(eps_vir.shape, F32),
            pltpu.VMEM((2 * NP + 8, 128), jnp.int32),
            pltpu.SMEM((2 * NP + 8, 128), jnp.int32),
            pltpu.VMEM((2 * capt * HALF, 128), F32),
            pltpu.VMEM((dead, TILE, 128), BF16),
            pltpu.VMEM((jdev, capt, area), BF16),
            pltpu.VMEM((NH, jdev, capt, area), BF16),
            pltpu.VMEM((2 * capt * HALF, 128), F32),
            pltpu.VMEM((SIDE, 2, QROWS, 128), BF16),
            pltpu.VMEM((SIDE, 2, QROWS, 128), BF16),
            pltpu.VMEM((NP, SIDE, QROWS, 128), BF16),
            pltpu.VMEM((capt, TILE, 128), BF16),
            pltpu.VMEM((3, capt, 128), BF16),
            pltpu.VMEM((NP, LIVE2 * HALF, 128), BF16),
            pltpu.VMEM((2, SIDE, RROWS, 128), BF16),
            pltpu.VMEM((2, SIDE, RROWS, 128), BF16),
            pltpu.VMEM((2, SIDE, HROWS, 128), BF16),
            pltpu.VMEM((2, SIDE, HROWS, 128), BF16),
            pltpu.VMEM((SIDE - 1, HROWS, 128), BF16),
            pltpu.VMEM((SIDE - 1, HROWS, 128), BF16),
            pltpu.VMEM((SIDE, HROWS, 128), BF16),
            pltpu.VMEM((SIDE, HROWS, 128), BF16),
            pltpu.VMEM((LIVE2, HALF, 128), F32),
            pltpu.VMEM((2 * capt * HALF, 128), F32),
            pltpu.VMEM((NR, 1, 128), F32),
            pltpu.VMEM((NP, 1, 128), F32),
            dma((8,)),
            dma((1,)),
            dma((SIDE - 1,)),
            dma((SIDE,)),
            dma((NR,)),
            dma((NP,)),
            dma((NP, SIDE - 1)),
            dma((NP, SIDE)),
            dma((NP,)),
            dma((NP,)),
            dma((2, SIDE)),
            dma((2, SIDE)),
            dma((2, SIDE)),
            dma((2, SIDE)),
            dma((2, SIDE)),
            dma((2, SIDE)),
            dma((2, SIDE)),
            dma((2, SIDE)),
            dma((SIDE - 1,)),
            dma((SIDE,)),
            dma((SIDE - 1,)),
            dma((SIDE,)),
            dma((NR + NP,)),
            dma((NR + NP,)),
        ],
        compiler_params=pltpu.CompilerParams(
            collective_id=0, has_side_effects=True, vmem_limit_bytes=60 << 20
        ),
    )(slab, eps_occ, amps[0], tile_index, ovov[0], ints, history[:, 0], eps_vir)
    return new_amps[None], gram[0, : NH + 1]


def solution(mesh):
    in_specs = (
        P("pair", "reorder", None, None),
        P(),
        P("pair", "reorder", None, None),
        P("pair", "reorder", None, None, None),
        P(None, "pair", "reorder", None, None),
        P(),
        P(),
        P(),
    )
    out_specs = (P("pair", "reorder", None, None), P())
    return jax.shard_map(local, mesh=mesh, in_specs=in_specs, out_specs=out_specs, check_vma=False)
```
